32 devices in a mesh: dp: 8 (over z, x), mp: 4 (over y, core).
Axes of the slice: x: 2, y: 2, z: 4, core: 2. Of those that a mesh axis runs over, the one named last changes fastest.
Arguments:
- encoder_input: bfloat16 [8, 1024, 768], P('dp'), may hold values from -6 to 6
- decoder_input: bfloat16 [8, 1024, 768], P('dp'), may hold values from -6 to 6
- encoder_lengths: int32 [8, 8], P('dp'), may hold values from 1 to 384, 1024 in all within a row
- decoder_lengths: int32 [8, 8], P('dp'), may hold values from 1 to 384, 1024 in all within a row
- encoder_buckets: int32 [2047], replicated, may hold values from 0 to 31
- decoder_buckets: int32 [1024], replicated, may hold values from 0 to 31
- encoder_attn_gain: float32 [768], replicated, may hold values from 0.5 to 1.5
- encoder_query: bfloat16 [768, 768], P(None, 'mp'), may hold values from -0.21875 to 0.21875
- encoder_key: bfloat16 [768, 768], P(None, 'mp'), may hold values from -0.21875 to 0.21875
- encoder_value: bfloat16 [768, 768], P(None, 'mp'), may hold values from -0.21875 to 0.21875
- encoder_output: bfloat16 [768, 768], P('mp'), may hold values from -0.75 to 0.75
- encoder_bias: float32 [32, 12], P(None, 'mp'), may hold values from -4 to 4
- encoder_ffn_gain: float32 [768], replicated, may hold values from 0.5 to 1.5
- encoder_ffn_in: bfloat16 [768, 3072], P(None, 'mp'), may hold values from -0.21875 to 0.21875
- encoder_ffn_out: bfloat16 [3072, 768], P('mp'), may hold values from -0.109375 to 0.109375
- decoder_attn_gain: float32 [768], replicated, may hold values from 0.5 to 1.5
- decoder_query: bfloat16 [768, 768], P(None, 'mp'), may hold values from -0.21875 to 0.21875
- decoder_key: bfloat16 [768, 768], P(None, 'mp'), may hold values from -0.21875 to 0.21875
- decoder_value: bfloat16 [768, 768], P(None, 'mp'), may hold values from -0.21875 to 0.21875
- decoder_output: bfloat16 [768, 768], P('mp'), may hold values from -0.75 to 0.75
- decoder_bias: float32 [32, 12], P(None, 'mp'), may hold values from -4 to 4
- cross_gain: float32 [768], replicated, may hold values from 0.5 to 1.5
- cross_query: bfloat16 [768, 768], P(None, 'mp'), may hold values from -0.21875 to 0.21875
- cross_key: bfloat16 [768, 768], P(None, 'mp'), may hold values from -0.21875 to 0.21875
- cross_value: bfloat16 [768, 768], P(None, 'mp'), may hold values from -0.21875 to 0.21875
- cross_output: bfloat16 [768, 768], P('mp'), may hold values from -0.75 to 0.75
- decoder_ffn_gain: float32 [768], replicated, may hold values from 0.5 to 1.5
- decoder_ffn_in: bfloat16 [768, 3072], P(None, 'mp'), may hold values from -0.21875 to 0.21875
- decoder_ffn_out: bfloat16 [3072, 768], P('mp'), may hold values from -0.109375 to 0.109375
- encoder_cotangent: bfloat16 [8, 1024, 768], P('dp'), may hold values from -6 to 6
- decoder_cotangent: bfloat16 [8, 1024, 768], P('dp'), may hold values from -6 to 6
Outputs:
- encoder_result: bfloat16 [8, 1024, 768], P('dp')
- decoder_result: bfloat16 [8, 1024, 768], P('dp')
- encoder_input_grad: float32 [8, 1024, 768], P('dp')
- decoder_input_grad: float32 [8, 1024, 768], P('dp')
- encoder_attn_gain_grad: float32 [768], replicated
- encoder_query_grad: float32 [768, 768], P(None, 'mp')
- encoder_key_grad: float32 [768, 768], P(None, 'mp')
- encoder_value_grad: float32 [768, 768], P(None, 'mp')
- encoder_output_grad: float32 [768, 768], P('mp')
- encoder_bias_grad: float32 [32, 12], P(None, 'mp')
- encoder_ffn_gain_grad: float32 [768], replicated
- encoder_ffn_in_grad: float32 [768, 3072], P(None, 'mp')
- encoder_ffn_out_grad: float32 [3072, 768], P('mp')
- decoder_attn_gain_grad: float32 [768], replicated
- decoder_query_grad: float32 [768, 768], P(None, 'mp')
- decoder_key_grad: float32 [768, 768], P(None, 'mp')
- decoder_value_grad: float32 [768, 768], P(None, 'mp')
- decoder_output_grad: float32 [768, 768], P('mp')
- decoder_bias_grad: float32 [32, 12], P(None, 'mp')
- cross_gain_grad: float32 [768], replicated
- cross_query_grad: float32 [768, 768], P(None, 'mp')
- cross_key_grad: float32 [768, 768], P(None, 'mp')
- cross_value_grad: float32 [768, 768], P(None, 'mp')
- cross_output_grad: float32 [768, 768], P('mp')
- decoder_ffn_gain_grad: float32 [768], replicated
- decoder_ffn_in_grad: float32 [768, 3072], P(None, 'mp')
- decoder_ffn_out_grad: float32 [3072, 768], P('mp')
The draws below stay inside these ranges and needn't reach their ends.
Inputs may be any that keep to these rules, and one draw needn't show every extreme that they name: `encoder_lengths`: each sequence's 8 source document lengths sum to 1024, and one of them is exactly 384. `decoder_lengths`: each sequence's 8 target document lengths sum to 1024, and one of them is exactly 384.
All inputs are finite; a program needn't handle non-finite values.
Results may differ from the reference program's by a relative error of at most 0.029.
Values sent between devices are 32-bit elements; how exact they have to be, the bound alone decides.
A program may use at most 320 MiB of HBM per device.

```python
import math
import jax
import jax.numpy as jnp
import numpy as np
from jax import lax

D = 768
H = 12
DK = 64
FF = 3072
NB = 32
INNER = 768
SEQ = 1024
DOCS = 8
MOST = 384
BATCH = 8


def set_ends(result, rng, smallest, largest):
    longest = result.shape.index(max(result.shape))
    spots = []
    for shift in (0, 1):
        where = [jax.random.randint(jax.random.fold_in(rng, axis), (), 0, length) for axis, length in enumerate(result.shape)]
        where[longest] = (where[longest] + shift) % result.shape[longest]
        spots.append(tuple(where))
    return result.at[spots[0]].set(smallest).at[spots[1]].set(largest)


def shard_levels(own_key, shape, shards, low, largest):
    def one(dim, blocks):
        heights = jax.random.uniform(jax.random.fold_in(jax.random.fold_in(own_key, 6), dim), (blocks,), jnp.float32, low / len(shards), largest / len(shards))
        return jnp.repeat(jnp.exp(heights), shape[dim] // blocks).reshape((-1,) + (1,) * (len(shape) - dim - 1))

    loudness = one(*shards[0])
    for cut in shards[1:]:
        loudness = loudness * one(*cut)
    return loudness


def profile(count, total, limit, lean):
    loads = [(1 << 20) // math.isqrt(rank ** lean) + 1 for rank in range(2, count + 1)]
    surplus, holding = total - limit - (count - 1), [1] * (count - 1)
    while surplus > 0:
        movable = [i for i in range(count - 1) if holding[i] < limit]
        whole, budget = sum([loads[i] for i in movable]), surplus
        for i in movable:
            more = min(limit - holding[i], max(1, budget * loads[i] // whole), surplus)
            holding[i] = holding[i] + more
            surplus = surplus - more
    return np.array([limit] + holding)


def uneven_parts(rng, number_of, total, reach, lean):
    if number_of == 2:
        one = jax.random.randint(rng, (), max(1, total - reach), min(reach, total - 1) + 1)
        return jnp.stack([one, total - one])
    sizes = jnp.asarray(profile(number_of, total, reach, lean), jnp.int32)
    twos = (number_of - 1) // 2
    source_of, taker = sizes[1:1 + 2 * twos:2], sizes[2:2 + 2 * twos:2]
    margin = jnp.minimum(source_of - 1, reach - taker)
    shifted = jax.random.randint(jax.random.fold_in(rng, 1), (twos,), 0, 1 << 20) % (margin + 1)
    sizes = sizes.at[1:1 + 2 * twos:2].set(source_of - shifted).at[2:2 + 2 * twos:2].set(taker + shifted)
    return sizes[jax.random.permutation(jax.random.fold_in(rng, 2), number_of)]


def scatter_about(rng, dims, spread, most, split=(), kind=jnp.bfloat16):
    drawn = spread * jax.random.normal(rng, dims, jnp.float32)
    if split:
        drawn = drawn * shard_levels(rng, dims, split, -0.22, 0.18)
    return jnp.clip(drawn, -most, most).astype(kind)


def setup_inputs(seed: int = 0) -> dict:
    splits = jax.random.split(jax.random.key(seed), 32)
    encoder_input = scatter_about(splits[0], (BATCH, SEQ, D), 1.0, 6.0, ((0, 8),))
    decoder_input = scatter_about(splits[1], (BATCH, SEQ, D), 1.0, 6.0, ((0, 8),))
    encoder_lengths = jax.vmap(lambda own: uneven_parts(own, DOCS, SEQ, MOST, 2))(jax.random.split(splits[2], BATCH)).reshape((BATCH, DOCS)).astype(jnp.int32)
    decoder_lengths = jax.vmap(lambda own: uneven_parts(own, DOCS, SEQ, MOST, 2))(jax.random.split(splits[3], BATCH)).reshape((BATCH, DOCS)).astype(jnp.int32)
    encoder_buckets = set_ends(jax.random.randint(splits[4], (2 * SEQ - 1,), 0, NB), jax.random.fold_in(splits[4], 1), 0, NB - 1).astype(jnp.int32)
    decoder_buckets = set_ends(jax.random.randint(splits[5], (SEQ,), 0, NB), jax.random.fold_in(splits[5], 1), 0, NB - 1).astype(jnp.int32)
    encoder_attn_gain = jnp.clip(1.0 + 0.1 * jax.random.normal(splits[6], (D,), jnp.float32), 0.5, 1.5)
    encoder_query = scatter_about(splits[7], (D, INNER), D ** -0.5, 0.21875, ((1, 4),))
    encoder_key = scatter_about(splits[8], (D, INNER), D ** -0.5, 0.21875, ((1, 4),))
    encoder_value = scatter_about(splits[9], (D, INNER), D ** -0.5, 0.21875, ((1, 4),))
    encoder_output = scatter_about(splits[10], (INNER, D), DK ** -0.5, 0.75, ((0, 4),))
    encoder_bias = scatter_about(splits[11], (NB, H), 1.0, 4.0, ((1, 4),), jnp.float32)
    encoder_ffn_gain = jnp.clip(1.0 + 0.1 * jax.random.normal(splits[12], (D,), jnp.float32), 0.5, 1.5)
    encoder_ffn_in = scatter_about(splits[13], (D, FF), D ** -0.5, 0.21875, ((1, 4),))
    encoder_ffn_out = scatter_about(splits[14], (FF, D), FF ** -0.5, 0.109375, ((0, 4),))
    decoder_attn_gain = jnp.clip(1.0 + 0.1 * jax.random.normal(splits[15], (D,), jnp.float32), 0.5, 1.5)
    decoder_query = scatter_about(splits[16], (D, INNER), D ** -0.5, 0.21875, ((1, 4),))
    decoder_key = scatter_about(splits[17], (D, INNER), D ** -0.5, 0.21875, ((1, 4),))
    decoder_value = scatter_about(splits[18], (D, INNER), D ** -0.5, 0.21875, ((1, 4),))
    decoder_output = scatter_about(splits[19], (INNER, D), DK ** -0.5, 0.75, ((0, 4),))
    decoder_bias = scatter_about(splits[20], (NB, H), 1.0, 4.0, ((1, 4),), jnp.float32)
    cross_gain = jnp.clip(1.0 + 0.1 * jax.random.normal(splits[21], (D,), jnp.float32), 0.5, 1.5)
    cross_query = scatter_about(splits[22], (D, INNER), D ** -0.5, 0.21875, ((1, 4),))
    cross_key = scatter_about(splits[23], (D, INNER), D ** -0.5, 0.21875, ((1, 4),))
    cross_value = scatter_about(splits[24], (D, INNER), D ** -0.5, 0.21875, ((1, 4),))
    cross_output = scatter_about(splits[25], (INNER, D), DK ** -0.5, 0.75, ((0, 4),))
    decoder_ffn_gain = jnp.clip(1.0 + 0.1 * jax.random.normal(splits[26], (D,), jnp.float32), 0.5, 1.5)
    decoder_ffn_in = scatter_about(splits[27], (D, FF), D ** -0.5, 0.21875, ((1, 4),))
    decoder_ffn_out = scatter_about(splits[28], (FF, D), FF ** -0.5, 0.109375, ((0, 4),))
    encoder_cotangent = scatter_about(splits[29], (BATCH, SEQ, D), 1.0, 6.0, ((0, 8),))
    decoder_cotangent = scatter_about(splits[30], (BATCH, SEQ, D), 1.0, 6.0, ((0, 8),))
    return dict(encoder_input=encoder_input, decoder_input=decoder_input, encoder_lengths=encoder_lengths, decoder_lengths=decoder_lengths, encoder_buckets=encoder_buckets, decoder_buckets=decoder_buckets, encoder_attn_gain=encoder_attn_gain, encoder_query=encoder_query, encoder_key=encoder_key, encoder_value=encoder_value, encoder_output=encoder_output, encoder_bias=encoder_bias, encoder_ffn_gain=encoder_ffn_gain, encoder_ffn_in=encoder_ffn_in, encoder_ffn_out=encoder_ffn_out, decoder_attn_gain=decoder_attn_gain, decoder_query=decoder_query, decoder_key=decoder_key, decoder_value=decoder_value, decoder_output=decoder_output, decoder_bias=decoder_bias, cross_gain=cross_gain, cross_query=cross_query, cross_key=cross_key, cross_value=cross_value, cross_output=cross_output, decoder_ffn_gain=decoder_ffn_gain, decoder_ffn_in=decoder_ffn_in, decoder_ffn_out=decoder_ffn_out, encoder_cotangent=encoder_cotangent, decoder_cotangent=decoder_cotangent)


EPS = 1e-06
NEG = -1e+30
HIGHEST = lax.Precision.HIGHEST

@jax.custom_vjp
def low(v):
    return lax.optimization_barrier(v.astype(jnp.bfloat16)).astype(jnp.float32)

@jax.custom_vjp
def low_back(v):
    return v

def low_keep(v):
    return (low(v), None)

def low_pass(kept, grad):
    return (grad,)

def back_keep(v):
    return (v, None)

def back_low(kept, grad):
    return (low(grad),)
low.defvjp(low_keep, low_pass)
low_back.defvjp(back_keep, back_low)

def round_both(value):
    return low_back(low(value))

def matmul(left, right):
    return jnp.dot(left, right, precision=HIGHEST)

def rms_norm(stream, gain):
    return stream * lax.rsqrt(lax.optimization_barrier(jnp.mean(stream * stream, axis=-1, keepdims=True)) + EPS) * gain

def doc_ids(lengths, seq_len):
    ends = jnp.cumsum(lengths, axis=-1).astype(jnp.int32)
    places = lax.broadcasted_iota(jnp.int32, lengths.shape[:-1] + (seq_len, lengths.shape[-1]), lengths.ndim - 1)
    return lax.optimization_barrier(jnp.sum((places >= ends[..., None, :]).astype(jnp.int32), axis=-1)).astype(jnp.int32)

def distance_table(buckets, table):
    onehot = (buckets[:, None] == jnp.arange(table.shape[0], dtype=jnp.int32)[None, :]).astype(jnp.float32)
    return jnp.dot(onehot, table, precision=HIGHEST)

def bias_rows(dist, start, count, keys, causal):
    rows = start + lax.broadcasted_iota(jnp.int32, (count, keys), 0)
    cols = lax.broadcasted_iota(jnp.int32, (count, keys), 1)
    if causal:
        index = jnp.maximum(rows - cols, 0)
    else:
        index = rows - cols + keys - 1
    return jnp.transpose(jnp.take(dist, index, axis=0), (2, 0, 1))

def attend(query_in, key_in, w_query, w_key, w_value, w_out, position, allowed):
    seq = query_in.shape[0]
    keys = key_in.shape[0]
    heads = w_query.shape[1] // DK
    queries = round_both(matmul(query_in, w_query)).reshape(seq, heads, DK)
    key_rows = round_both(matmul(key_in, w_key)).reshape(keys, heads, DK)
    value_rows = round_both(matmul(key_in, w_value)).reshape(keys, heads, DK)
    scores = jnp.einsum('qhd,khd->hqk', queries, key_rows, precision=HIGHEST) * DK ** (-0.5)
    if position is not None:
        scores = scores + position
    scores = jnp.where(allowed[None], low_back(scores), NEG)
    attn_probs = low(jax.nn.softmax(scores, axis=-1))
    attended = jnp.einsum('hqk,khd->qhd', attn_probs, value_rows, precision=HIGHEST).reshape(seq, heads * DK)
    attended = round_both(attended)
    return low_back(matmul(attended, w_out))

def feed_forward(stream, gain, w_in, w_out):
    normed = low(rms_norm(stream, gain))
    hidden = low_back(matmul(normed, w_in))
    active = low(jax.nn.gelu(hidden, approximate=True))
    return stream + low_back(matmul(active, w_out))

def layers_row(params, encoder_row, decoder_row, enc_docs, dec_docs, encoder_buckets, decoder_buckets):
    enc_attn_gain, enc_query, enc_key, enc_value, enc_output, enc_bias, enc_ffn_gain, enc_ffn_in, enc_ffn_out, dec_attn_gain, dec_query, dec_key, dec_value, dec_output, dec_bias, cross_gain, cross_query, cross_key, cross_value, cross_output, dec_ffn_gain, dec_ffn_in, dec_ffn_out = params
    seq = encoder_row.shape[0]
    rows = lax.broadcasted_iota(jnp.int32, (seq, seq), 0)
    cols = lax.broadcasted_iota(jnp.int32, (seq, seq), 1)
    enc_mask = enc_docs[:, None] == enc_docs[None, :]
    self_mask = (dec_docs[:, None] == dec_docs[None, :]) & (cols <= rows)
    cross_mask = dec_docs[:, None] == enc_docs[None, :]
    enc_pos = bias_rows(distance_table(encoder_buckets, enc_bias), 0, seq, seq, False)
    dec_pos = bias_rows(distance_table(decoder_buckets, dec_bias), 0, seq, seq, True)
    normed = low(rms_norm(encoder_row, enc_attn_gain))
    stream = encoder_row + attend(normed, normed, enc_query, enc_key, enc_value, enc_output, enc_pos, enc_mask)
    encoder_out = feed_forward(stream, enc_ffn_gain, enc_ffn_in, enc_ffn_out)
    memory = low(encoder_out)
    normed = low(rms_norm(decoder_row, dec_attn_gain))
    stream = decoder_row + attend(normed, normed, dec_query, dec_key, dec_value, dec_output, dec_pos, self_mask)
    normed = low(rms_norm(stream, cross_gain))
    stream = stream + attend(normed, memory, cross_query, cross_key, cross_value, cross_output, None, cross_mask)
    decoder_out = feed_forward(stream, dec_ffn_gain, dec_ffn_in, dec_ffn_out)
    return (encoder_out, decoder_out)

def reference(encoder_input, decoder_input, encoder_lengths, decoder_lengths, encoder_buckets, decoder_buckets, encoder_attn_gain, encoder_query, encoder_key, encoder_value, encoder_output, encoder_bias, encoder_ffn_gain, encoder_ffn_in, encoder_ffn_out, decoder_attn_gain, decoder_query, decoder_key, decoder_value, decoder_output, decoder_bias, cross_gain, cross_query, cross_key, cross_value, cross_output, decoder_ffn_gain, decoder_ffn_in, decoder_ffn_out, encoder_cotangent, decoder_cotangent):
    weights = (encoder_attn_gain, encoder_query, encoder_key, encoder_value, encoder_output, encoder_bias, encoder_ffn_gain, encoder_ffn_in, encoder_ffn_out, decoder_attn_gain, decoder_query, decoder_key, decoder_value, decoder_output, decoder_bias, cross_gain, cross_query, cross_key, cross_value, cross_output, decoder_ffn_gain, decoder_ffn_in, decoder_ffn_out)
    params = tuple((weight.astype(jnp.float32) for weight in weights))
    enc_docs = doc_ids(encoder_lengths, SEQ)
    dec_docs = doc_ids(decoder_lengths, SEQ)

    def step(carry, row):
        encoder_row, decoder_row, enc_row_docs, dec_row_docs, enc_cot, dec_cot = row

        def forward(values, enc_in, dec_in):
            return layers_row(values, enc_in, dec_in, enc_row_docs, dec_row_docs, encoder_buckets, decoder_buckets)
        outputs, pullback = jax.vjp(forward, params, encoder_row, decoder_row)
        grads = pullback((enc_cot, dec_cot))
        carry = jax.tree.map(lambda total, part: total + part, carry, grads[0])
        return (carry, (outputs[0].astype(jnp.bfloat16), outputs[1].astype(jnp.bfloat16), grads[1], grads[2]))
    zeros = jax.tree.map(jnp.zeros_like, params)
    sequences = (encoder_input.astype(jnp.float32), decoder_input.astype(jnp.float32), enc_docs, dec_docs, encoder_cotangent.astype(jnp.float32), decoder_cotangent.astype(jnp.float32))
    totals, stacked = lax.scan(step, zeros, sequences)
    return (stacked[0], stacked[1], stacked[2], stacked[3], totals[0], totals[1], totals[2], totals[3], totals[4], totals[5], totals[6], totals[7], totals[8], totals[9], totals[10], totals[11], totals[12], totals[13], totals[14], totals[15], totals[16], totals[17], totals[18], totals[19], totals[20], totals[21], totals[22])
```

```python
import functools

import jax
import jax.numpy as jnp
from jax import lax
from jax.experimental import pallas as pl
from jax.experimental.pallas import tpu as pltpu
from jax.sharding import PartitionSpec as P

DK = 64
EPS = 1e-06
NEG = -1e30
HIGHEST = lax.Precision.HIGHEST
TILE = 128
BQ = 256
KC = 128
SPEEDUP = 1 << 20
VMEM_BYTES = 60 * 1024 * 1024


def doc_ends(lens_ref):
    ends = []
    total = jnp.int32(0)
    for j in range(lens_ref.shape[1]):
        total = total + lens_ref[0, j]
        ends.append(total)
    return ends


def docs_at(places, ends):
    result = jnp.zeros(places.shape, jnp.int32)
    for end in ends:
        result = result + (places >= end).astype(jnp.int32)
    return result


def key_range(ql_ref, q_ends, kl_ref, block, causal):
    first = block * BQ
    last = first + BQ - 1
    low = jnp.int32(0)
    high = jnp.int32(0)
    for j, end in enumerate(q_ends):
        low = low + jnp.where(end <= first, kl_ref[0, j], 0)
        high = high + jnp.where(end - ql_ref[0, j] <= last, kl_ref[0, j], 0)
    if causal:
        high = jnp.minimum(high, first + BQ)
    return low // KC, (high + KC - 1) // KC


def bucket_hits(buckets_ref, count):
    ids = lax.broadcasted_iota(jnp.int32, (count, buckets_ref.shape[1]), 0)
    return ids == buckets_ref[...]


def make_tiles(buckets_ref, table_ref, tiles_ref):
    hits = bucket_hits(buckets_ref, table_ref.shape[0])
    width = buckets_ref.shape[1]
    for h in range(tiles_ref.shape[0]):
        row = jnp.sum(jnp.where(hits, table_ref[:, h : h + 1], 0.0), axis=0, keepdims=True)
        row = jnp.where(buckets_ref[...] < 0, NEG, row)
        for k in range(tiles_ref.shape[1] // TILE):
            start = width - 2 * TILE - k * TILE
            window = jnp.broadcast_to(row[:, start : start + 2 * TILE], (TILE, 2 * TILE))
            skewed = pltpu.roll(window, 0, 1, stride=1, stride_axis=0)
            tiles_ref[h, k * TILE : (k + 1) * TILE, :] = skewed[:, TILE:]


def sum_tiles(buckets_ref, grad_tiles_ref, grad_table_ref):
    count = grad_table_ref.shape[0]
    width = buckets_ref.shape[1]
    hits = bucket_hits(buckets_ref, count)
    blocks = grad_tiles_ref.shape[1] // TILE
    blank = jnp.zeros((8, TILE), jnp.float32)
    for h in range(grad_tiles_ref.shape[0]):
        halves = []
        for k in range(blocks):
            total = jnp.zeros((8, 2 * TILE), jnp.float32)
            for a in range(0, TILE, 8):
                piece = grad_tiles_ref[h, k * TILE + a : k * TILE + a + 8, :]
                wide = jnp.concatenate([blank, piece], axis=1)
                total = total + pltpu.roll(wide, (2 * TILE - a) % (2 * TILE), 1)
            halves.append(total)
        parts = []
        for m in range(width // TILE):
            upper = halves[blocks - 1 - m][:, :TILE] if m < blocks else None
            lower = halves[blocks - m][:, TILE:] if m >= 1 else None
            part = upper if lower is None else lower if upper is None else upper + lower
            parts.append(part)
        group = jnp.concatenate(parts, axis=1)
        row = group[0:1]
        for b in range(1, 8):
            row = row + pltpu.roll(group[b : b + 1], width - b, 1)
        grad_table_ref[:, h : h + 1] = jnp.sum(jnp.where(hits, row, 0.0), axis=1, keepdims=True)


def tile_rows(tiles_ref, h, block, chunk, keys):
    parts = []
    for t in range(BQ // TILE):
        start = keys - TILE - TILE * (block * (BQ // TILE) + t) + chunk * KC
        parts.append(tiles_ref[h, pl.ds(pl.multiple_of(start, TILE), KC), :])
    return jnp.concatenate(parts, axis=1)


def head_mask(h, width):
    lane = lax.broadcasted_iota(jnp.int32, (1, width), 1)
    return ((lane >= h * DK) & (lane < (h + 1) * DK)).astype(jnp.bfloat16)


def dot_last(left, right):
    return lax.dot_general(
        left, right, (((1,), (1,)), ((), ())), preferred_element_type=jnp.float32
    )


def dot(left, right):
    return jnp.dot(left, right, preferred_element_type=jnp.float32)


def flip(value):
    return jnp.transpose(value.astype(jnp.float32)).astype(value.dtype)


ROWS = 256


def ref_norm(stream, gain):
    scale = lax.rsqrt(jnp.mean(stream * stream, axis=-1, keepdims=True) + EPS)
    return stream * scale * gain


def norm_back(stream, gain, grad_normed):
    scale = lax.rsqrt(jnp.mean(stream * stream, axis=-1, keepdims=True) + EPS)
    unit = stream * scale
    scaled = gain * grad_normed
    grad = scale * (scaled - unit * jnp.mean(scaled * unit, axis=-1, keepdims=True))
    return grad, jnp.sum(grad_normed * unit, axis=0, keepdims=True)


GELU_SCALE = 0.7978845608028654
GELU_CUBE = 0.044715


def gelu_parts(value):
    square = value * value
    curve = jnp.tanh(GELU_SCALE * (value + GELU_CUBE * value * square))
    active = 0.5 * value * (1.0 + curve)
    slope = 0.5 * (1.0 + curve) + 0.5 * value * (1.0 - curve * curve) * GELU_SCALE * (
        1.0 + 3.0 * GELU_CUBE * square
    )
    return active, slope


def block_rows(index):
    return pl.ds(pl.multiple_of(index * ROWS, ROWS), ROWS)


def attend_block(block, causal, biased, ql_ref, kl_ref, q_block, k_ref, vt_ref, kd_ref, s_ref, o_acc, tiles_ref, lse_ref):
    keys, width = k_ref.shape
    heads = width // DK
    q_ends = doc_ends(ql_ref)
    q_docs = docs_at(block * BQ + lax.broadcasted_iota(jnp.int32, (1, BQ), 1), q_ends)
    queries = q_block * jnp.bfloat16(DK ** (-0.5))
    masked = [queries * head_mask(h, width) for h in range(heads)]
    low, high = key_range(ql_ref, q_ends, kl_ref, block, causal)

    def first(chunk, tops):
        rows = pl.ds(pl.multiple_of(chunk * KC, KC), KC)
        docs = jnp.concatenate([kd_ref[rows, :]] * (BQ // TILE), axis=1)
        allowed = docs == q_docs
        fresh = []
        for h in range(heads):
            scores = dot_last(k_ref[rows, :], masked[h])
            if biased:
                scores = scores + tile_rows(tiles_ref, h, block, chunk, keys)
            scores = jnp.where(allowed, scores, NEG)
            s_ref[h, rows, :] = scores
            fresh.append(jnp.maximum(tops[h], jnp.max(scores, axis=0, keepdims=True)))
        return tuple(fresh)

    tops = lax.fori_loop(
        low, high, first, tuple(jnp.full((1, BQ), NEG, jnp.float32) for _ in range(heads))
    )
    o_acc[...] = jnp.zeros_like(o_acc)

    def second(chunk, totals):
        rows = pl.ds(pl.multiple_of(chunk * KC, KC), KC)
        fresh = []
        for h in range(heads):
            probs = jnp.exp(s_ref[h, rows, :] - tops[h])
            fresh.append(totals[h] + jnp.sum(probs, axis=0, keepdims=True))
            o_acc[h * DK : (h + 1) * DK, :] += dot(
                vt_ref[h * DK : (h + 1) * DK, rows], probs.astype(jnp.bfloat16)
            )
        return tuple(fresh)

    totals = lax.fori_loop(
        low, high, second, tuple(jnp.zeros((1, BQ), jnp.float32) for _ in range(heads))
    )
    outs = []
    for h in range(heads):
        lse_ref[h : h + 1, :] = tops[h] + jnp.log(totals[h])
        outs.append(o_acc[h * DK : (h + 1) * DK, :] / totals[h])
    return jnp.concatenate(outs, axis=0).astype(jnp.bfloat16).astype(jnp.float32)


def put_out(out, o_ref, ot_ref):
    o_ref[...] = jnp.transpose(out).astype(jnp.bfloat16)
    ot_ref[...] = out


def order_pieces(me, own, far, sib, sibfar, target_ref):
    other = lax.rem(me + 2, 4)
    beside = me + 1 - 2 * lax.rem(me, 2)
    target_ref[me] = own
    target_ref[other] = far
    target_ref[beside] = sib
    target_ref[lax.rem(beside + 2, 4)] = sibfar


def order_weights(me, refs, target_ref):
    order_pieces(me, *[ref[...].astype(jnp.bfloat16) for ref in refs], target_ref)


def out_product(me, refs, lanes, weights_ref, pieces_ref):
    order_pieces(me, *[ref[:, lanes] for ref in refs], pieces_ref)
    total = None
    for m in range(4):
        left = jnp.transpose(pieces_ref[m]).astype(jnp.bfloat16)
        product = dot(left, weights_ref[m])
        total = product if total is None else total + product
    return total


def self_forward_kernel(causal, *refs):
    ql_ref, x_ref, gain_ref, wq_ref, wk_ref, wv_ref, buckets_ref, table_ref = refs[:8]
    n_ref, q_ref, k_ref, v_ref, o_ref, lse_ref = refs[8:14]
    ot_ref = refs[14]
    vt_ref, kd_ref, s_ref, o_acc, tiles_ref = refs[15:]
    block = pl.program_id(0)
    keys = k_ref.shape[0]

    @pl.when(block == 0)
    def _():
        for b in range(keys // ROWS):
            rows = slice(b * ROWS, (b + 1) * ROWS)
            normed = ref_norm(x_ref[rows, :].astype(jnp.float32), gain_ref[...]).astype(
                jnp.bfloat16
            )
            n_ref[rows, :] = normed
            q_ref[rows, :] = dot_last(normed, wq_ref[...]).astype(jnp.bfloat16)
            k_ref[rows, :] = dot_last(normed, wk_ref[...]).astype(jnp.bfloat16)
            value = dot_last(normed, wv_ref[...])
            v_ref[rows, :] = value.astype(jnp.bfloat16)
            vt_ref[:, rows] = jnp.transpose(value).astype(jnp.bfloat16)
        kd_ref[...] = docs_at(
            lax.broadcasted_iota(jnp.int32, (keys, TILE), 0), doc_ends(ql_ref)
        )
        make_tiles(buckets_ref, table_ref, tiles_ref)

    out = attend_block(
        block, causal, True, ql_ref, ql_ref, q_ref[block_rows(block), :],
        k_ref, vt_ref, kd_ref, s_ref, o_acc, tiles_ref, lse_ref,
    )
    put_out(out, o_ref, ot_ref)


def cross_forward_kernel(*refs):
    me_ref, ql_ref, kl_ref, y0_ref = refs[:4]
    dec_pieces, dec_weights = refs[4:8], refs[8:12]
    x1_ref, enc_sum_ref, gain_ref, wq_ref, wk_ref, wv_ref = refs[12:18]
    y1_ref, n_ref, memory_ref, q_ref, k_ref, v_ref, o_ref, lse_ref, ot_ref = refs[18:27]
    vt_ref, kd_ref, s_ref, o_acc, weights_ref, pieces_ref = refs[27:]
    block = pl.program_id(0)
    keys = k_ref.shape[0]
    me = me_ref[0]

    @pl.when(block == 0)
    def _():
        for b in range(keys // ROWS):
            rows = slice(b * ROWS, (b + 1) * ROWS)
            memory = (x1_ref[rows, :] + enc_sum_ref[rows, :]).astype(jnp.bfloat16)
            memory_ref[rows, :] = memory
            k_ref[rows, :] = dot_last(memory, wk_ref[...]).astype(jnp.bfloat16)
            value = dot_last(memory, wv_ref[...])
            v_ref[rows, :] = value.astype(jnp.bfloat16)
            vt_ref[:, rows] = jnp.transpose(value).astype(jnp.bfloat16)
        kd_ref[...] = docs_at(
            lax.broadcasted_iota(jnp.int32, (keys, TILE), 0), doc_ends(kl_ref)
        )
        order_weights(me, dec_weights, weights_ref)

    summed = out_product(me, dec_pieces, slice(None), weights_ref, pieces_ref)
    stream = y0_ref[...].astype(jnp.float32) + summed
    y1_ref[...] = stream
    normed = ref_norm(stream, gain_ref[...]).astype(jnp.bfloat16)
    n_ref[...] = normed
    queries = dot_last(normed, wq_ref[...]).astype(jnp.bfloat16)
    q_ref[...] = queries
    out = attend_block(
        block, False, False, ql_ref, kl_ref, queries,
        k_ref, vt_ref, kd_ref, s_ref, o_acc, None, lse_ref,
    )
    put_out(out, o_ref, ot_ref)


def ffn_forward_kernel(*refs):
    me_ref, x_ref = refs[:2]
    pieces, weights = refs[2:6], refs[6:10]
    gain_ref, wi_ref, wo_ref, x1_ref, n_ref, hid_ref, act_ref, part_ref = refs[10:18]
    weights_ref, pieces_ref = refs[18:]
    me = me_ref[0]

    @pl.when(pl.program_id(0) == 0)
    def _():
        order_weights(me, weights, weights_ref)

    summed = out_product(me, pieces, slice(None), weights_ref, pieces_ref)
    stream = x_ref[...].astype(jnp.float32) + summed
    x1_ref[...] = stream
    normed = ref_norm(stream, gain_ref[...]).astype(jnp.bfloat16)
    n_ref[...] = normed
    hidden = dot(normed, wi_ref[...])
    hid_ref[...] = hidden
    active = gelu_parts(hidden)[0].astype(jnp.bfloat16)
    act_ref[...] = active
    part_ref[...] = dot(active, wo_ref[...])


def ffn_both_kernel(*refs):
    me_ref, y_ref = refs[:2]
    pieces, weights = refs[2:6], refs[6:10]
    gain_ref, wi_ref, wo_ref, cot_ref = refs[10:14]
    y2_ref, n_ref, act_ref, dhid_ref, part_ref, out_part_ref, weights_ref, pieces_ref = refs[14:]
    me = me_ref[0]

    @pl.when(pl.program_id(0) == 0)
    def _():
        order_weights(me, weights, weights_ref)

    summed = out_product(me, pieces, slice(None), weights_ref, pieces_ref)
    stream = y_ref[...] + summed
    y2_ref[...] = stream
    normed = ref_norm(stream, gain_ref[...]).astype(jnp.bfloat16)
    n_ref[...] = normed
    active, slope = gelu_parts(dot(normed, wi_ref[...]))
    active = active.astype(jnp.bfloat16)
    act_ref[...] = active
    grad = (slope * dot_last(cot_ref[...], wo_ref[...])).astype(jnp.bfloat16)
    dhid_ref[...] = grad
    part_ref[...] = dot_last(grad, wi_ref[...])
    out_part_ref[...] = dot(active, wo_ref[...])


def ffn_backward_kernel(cot_ref, sum_ref, hid_ref, wi_ref, wo_ref, x_ref, g_ref, dhid_ref, part_ref):
    stream = cot_ref[...].astype(jnp.float32) + sum_ref[...]
    x_ref[...] = stream
    branch = stream.astype(jnp.bfloat16)
    g_ref[...] = branch
    slope = gelu_parts(hid_ref[...])[1]
    grad = (slope * dot_last(branch, wo_ref[...])).astype(jnp.bfloat16)
    dhid_ref[...] = grad
    part_ref[...] = dot_last(grad, wi_ref[...])


def half_rows(core, block, mine_ref, sib_ref):
    local = block_rows(lax.rem(block, 2))
    return jnp.where(block // 2 == core, mine_ref[local, :], sib_ref[local, :])


def piece_rows(core, block, refs):
    near, far, near_sib, far_sib = refs
    return half_rows(core, block, near, near_sib) + half_rows(core, block, far, far_sib)


def closing_kernel(x0_ref, eb_ref, egain_ref, z_ref, y0_ref, sb_ref, dgain_ref, s_ref, y2_ref, l_ref,
                   enc_ref, dec_ref, result_ref):
    for start, stream, gain, summed, out in (
        (x0_ref, eb_ref, egain_ref, z_ref, enc_ref), (y0_ref, sb_ref, dgain_ref, s_ref, dec_ref)
    ):
        grad, _ = norm_back(start[...].astype(jnp.float32), gain[...], summed[...])
        out[...] = stream[...] + grad
    result_ref[...] = (y2_ref[...] + l_ref[...]).astype(result_ref.dtype)


def attention_back_kernel(causal, biased, pieces, *refs):
    refs = list(refs)
    take = lambda n: [refs.pop(0) for _ in range(n)]
    core_ref, ql_ref, kl_ref = take(3)
    base_ref, stream_ref = take(2)
    dn_refs = take(pieces)
    gain_ref, wo_ref, q_ref, k_ref, v_ref, o_ref, lse_ref, wq_ref, wk_ref, wv_ref = take(10)
    buckets_ref, table_ref, x0_ref = take(3) if biased else (None, None, None)
    x_ref, g_ref, dq_ref, dk_ref, dv_ref, gain_grad_ref = take(6)
    if biased:
        dtable_ref, own_gain_ref = take(2)
    part_ref = take(1)[0]
    memory_part_ref = None if biased else take(1)[0]
    kt_ref, kd_ref, dq_acc, dk_acc, dv_acc = take(5)
    tiles_ref, grad_ref = take(2) if biased else (None, None)
    block = pl.program_id(0)
    keys, width = k_ref.shape
    heads = width // DK
    core = core_ref[0]
    q_ends = doc_ends(ql_ref)
    scale = jnp.bfloat16(DK ** (-0.5))

    @pl.when(block == 0)
    def _():
        kt_ref[...] = flip(k_ref[...])
        kd_ref[...] = docs_at(
            lax.broadcasted_iota(jnp.int32, (keys, TILE), 0), doc_ends(kl_ref)
        )
        dk_acc[...] = jnp.zeros_like(dk_acc)
        dv_acc[...] = jnp.zeros_like(dv_acc)
        gain_grad_ref[...] = jnp.zeros_like(gain_grad_ref)
        if biased:
            make_tiles(buckets_ref, table_ref, tiles_ref)
            grad_ref[...] = jnp.zeros_like(grad_ref)

    if pieces == 1:
        grad_normed = dn_refs[0][...]
    else:
        grad_normed = piece_rows(core, block, dn_refs)
    grad_in, gain_grad = norm_back(stream_ref[...], gain_ref[...], grad_normed)
    gain_grad_ref[...] += gain_grad
    grad_stream = base_ref[...].astype(jnp.float32) + grad_in
    x_ref[...] = grad_stream
    branch = grad_stream.astype(jnp.bfloat16)
    g_ref[...] = branch
    grads = dot_last(branch, wo_ref[...]).astype(jnp.bfloat16)

    q_docs = docs_at(block * BQ + lax.broadcasted_iota(jnp.int32, (1, BQ), 1), q_ends)
    queries = q_ref[...] * scale
    product = grads.astype(jnp.float32) * o_ref[...].astype(jnp.float32)
    pick = jnp.concatenate(
        [head_mask(h, width).astype(jnp.float32) for h in range(heads)]
        + [jnp.zeros((8 - heads, width), jnp.float32)],
        axis=0,
    )
    inner = lax.dot_general(
        pick,
        product,
        (((1,), (1,)), ((), ())),
        precision=HIGHEST,
        preferred_element_type=jnp.float32,
    )
    q_masked = [queries * head_mask(h, width) for h in range(heads)]
    g_masked = [grads * head_mask(h, width) for h in range(heads)]
    low, high = key_range(ql_ref, q_ends, kl_ref, block, causal)
    dq_acc[...] = jnp.zeros_like(dq_acc)

    @pl.loop(low, high)
    def _(chunk):
        rows = pl.ds(pl.multiple_of(chunk * KC, KC), KC)
        docs = jnp.concatenate([kd_ref[rows, :]] * (BQ // TILE), axis=1)
        allowed = docs == q_docs
        dk = dk_acc[rows, :]
        dv = dv_acc[rows, :]
        for h in range(heads):
            scores = dot_last(k_ref[rows, :], q_masked[h])
            if biased:
                scores = scores + tile_rows(tiles_ref, h, block, chunk, keys)
            scores = jnp.where(allowed, scores, NEG)
            probs = jnp.exp(scores - lse_ref[h : h + 1, :])
            grad_probs = dot_last(v_ref[rows, :], g_masked[h])
            grad_scores = (probs * (grad_probs - inner[h : h + 1, :])).astype(jnp.bfloat16)
            dv = dv + dot(probs.astype(jnp.bfloat16), g_masked[h])
            dk = dk + dot(grad_scores, q_masked[h])
            dq_acc[h * DK : (h + 1) * DK, :] += dot(
                kt_ref[h * DK : (h + 1) * DK, rows], grad_scores
            )
            if biased:
                for t in range(BQ // TILE):
                    start = keys - TILE - TILE * (block * (BQ // TILE) + t) + chunk * KC
                    piece = pl.ds(pl.multiple_of(start, TILE), KC)
                    grad_ref[h, piece, :] += grad_scores[:, t * TILE : (t + 1) * TILE].astype(
                        jnp.float32
                    )
        dk_acc[rows, :] = dk
        dv_acc[rows, :] = dv

    dq = (jnp.transpose(dq_acc[...]) * DK ** (-0.5)).astype(jnp.bfloat16)
    dq_ref[block_rows(block), :] = dq

    @pl.when(block == pl.num_programs(0) - 1)
    def _():
        dk_ref[...] = dk_acc[...].astype(jnp.bfloat16)
        dv_ref[...] = dv_acc[...].astype(jnp.bfloat16)
        own_gain = jnp.zeros(gain_grad_ref.shape, jnp.float32)
        for b in range(keys // ROWS):
            rows = slice(b * ROWS, (b + 1) * ROWS)
            from_q = dot(dq_ref[rows, :], wq_ref[...])
            from_kv = dot(dk_ref[rows, :], wk_ref[...]) + dot(
                dv_ref[rows, :], wv_ref[...]
            )
            if not biased:
                part_ref[rows, :] = from_q
                memory_part_ref[rows, :] = from_kv
                continue
            total = from_q + from_kv
            part_ref[rows, :] = total
            start = x0_ref[rows, :].astype(jnp.float32)
            unit = start * lax.rsqrt(jnp.mean(start * start, axis=-1, keepdims=True) + EPS)
            own_gain = own_gain + jnp.sum(total * unit, axis=0, keepdims=True)
        if biased:
            own_gain_ref[...] = own_gain
            sum_tiles(buckets_ref, grad_ref, dtable_ref)


def whole(shape):
    return pl.BlockSpec(shape, lambda *_: (0,) * len(shape), pipeline_mode=pl.Buffered(1))


def rows_spec(width):
    return pl.BlockSpec((BQ, width), lambda i: (i, 0))


def lanes_spec():
    return pl.BlockSpec((8, BQ), lambda i: (0, i))


SMEM_SPEC = pl.BlockSpec(memory_space=pltpu.SMEM)
BF16, F32 = jnp.bfloat16, jnp.float32


def call(kernel, name, grid, inputs, outputs, scratch, flops, exps=0):
    def size(shape, dtype):
        count = 1
        for dim in shape:
            count *= dim
        return count * jnp.dtype(dtype).itemsize

    moved = sum(size(a.shape, a.dtype) for a, _ in inputs) + sum(size(s, d) for s, d, _ in outputs)
    return pl.pallas_call(
        kernel,
        grid=grid,
        in_specs=[spec for _, spec in inputs],
        out_specs=[spec for _, _, spec in outputs],
        out_shape=[jax.ShapeDtypeStruct(shape, dtype) for shape, dtype, _ in outputs],
        scratch_shapes=scratch,
        compiler_params=pltpu.CompilerParams(
            dimension_semantics=("arbitrary",) * len(grid), vmem_limit_bytes=VMEM_BYTES
        ),
        cost_estimate=pl.CostEstimate(flops=flops // SPEEDUP, bytes_accessed=moved // SPEEDUP, transcendentals=exps // SPEEDUP),
        name=name,
    )(*[a for a, _ in inputs])


def full(array):
    return (array, whole(array.shape))


def attention_scratch(width, keys, biased):
    heads = width // DK
    scratch = [
        pltpu.VMEM((width, keys), BF16),
        pltpu.VMEM((keys, TILE), jnp.int32),
        pltpu.VMEM((heads, keys, BQ), F32),
        pltpu.VMEM((width, BQ), F32),
    ]
    if biased:
        scratch.append(pltpu.VMEM((heads, 2 * keys - TILE, TILE), F32))
    return scratch


def transposed_spec(width):
    return pl.BlockSpec((width, BQ), lambda i: (0, i))


def self_forward(lens, x, gain, wq, wk, wv, bias, causal, name):
    seq, model = x.shape
    width = wq.shape[0]
    inputs = [(lens, SMEM_SPEC)]
    inputs += [full(a) for a in (x, gain, wq, wk, wv, bias[0], bias[1])]
    outputs = [((seq, model), BF16, whole((seq, model)))]
    outputs += [((seq, width), BF16, whole((seq, width)))] * 3
    outputs += [((seq, width), BF16, rows_spec(width)), ((8, seq), F32, lanes_spec())]
    outputs.append(((width, seq), F32, transposed_spec(width)))
    result = call(
        functools.partial(self_forward_kernel, causal), name, (seq // BQ,), inputs, outputs,
        attention_scratch(width, seq, True), 6 * seq * model * width + 2 * seq * seq * width,
        seq * seq,
    )
    return result[:6], result[6]


def order_scratch(width, model, rows):
    return [pltpu.VMEM((4, width, model), BF16), pltpu.VMEM((4, width, rows), F32)]


def piece_inputs(pieces, weights):
    width = pieces[0].shape[0]
    return [(a, transposed_spec(width)) for a in pieces] + [full(a) for a in weights]


def cross_forward(me, ql, kl, y0, pieces, weights, x1, enc_sum, gain, wq, wk, wv):
    seq, model = y0.shape
    width = wq.shape[0]
    inputs = [(me, SMEM_SPEC), (ql, SMEM_SPEC), (kl, SMEM_SPEC), (y0, rows_spec(model))]
    inputs += piece_inputs(pieces, weights)
    inputs += [full(a) for a in (x1, enc_sum, gain, wq, wk, wv)]
    outputs = [
        ((seq, model), F32, rows_spec(model)),
        ((seq, model), BF16, rows_spec(model)),
        ((seq, model), BF16, whole((seq, model))),
        ((seq, width), BF16, rows_spec(width)),
        ((seq, width), BF16, whole((seq, width))),
        ((seq, width), BF16, whole((seq, width))),
        ((seq, width), BF16, rows_spec(width)),
        ((8, seq), F32, lanes_spec()),
        ((width, seq), F32, transposed_spec(width)),
    ]
    scratch = attention_scratch(width, seq, False) + order_scratch(width, model, ROWS)
    result = call(
        cross_forward_kernel, "cross_forward", (seq // BQ,), inputs, outputs, scratch,
        14 * seq * model * width + 2 * seq * seq * width, seq * seq,
    )
    return result[:8], result[8]


def row_outputs(seq, *kinds):
    return [((seq, width), dtype, rows_spec(width)) for width, dtype in kinds]


def ffn_forward(me, x, pieces, weights, gain, wi, wo):
    seq, model = x.shape
    units = wi.shape[1]
    inputs = [(me, SMEM_SPEC), (x, rows_spec(model))] + piece_inputs(pieces, weights)
    inputs += [full(a) for a in (gain, wi, wo)]
    outputs = row_outputs(seq, (model, F32), (model, BF16), (units, F32), (units, BF16), (model, F32))
    return call(
        ffn_forward_kernel, "ffn_forward", (seq // ROWS,), inputs, outputs,
        order_scratch(weights[0].shape[0], model, ROWS), 6 * seq * model * units, seq * units,
    )


def ffn_both(me, y, pieces, weights, gain, wi, wo, cot):
    seq, model = y.shape
    units = wi.shape[1]
    inputs = [(me, SMEM_SPEC), (y, rows_spec(model))] + piece_inputs(pieces, weights)
    inputs += [full(a) for a in (gain, wi, wo)] + [(cot, rows_spec(model))]
    outputs = row_outputs(
        seq, (model, F32), (model, BF16), (units, BF16), (units, BF16), (model, F32), (model, F32)
    )
    return call(
        ffn_both_kernel, "ffn_both", (seq // ROWS,), inputs, outputs,
        order_scratch(weights[0].shape[0], model, ROWS), 10 * seq * model * units, seq * units,
    )


def ffn_backward(cot, summed, hid, wi, wo):
    seq, units = hid.shape
    model = wi.shape[0]
    inputs = [(cot, rows_spec(model)), (summed, rows_spec(model)), (hid, rows_spec(units))]
    inputs += [full(wi), full(wo)]
    outputs = row_outputs(seq, (model, F32), (model, BF16), (units, BF16), (model, F32))
    return call(
        ffn_backward_kernel, "ffn_backward", (seq // ROWS,), inputs, outputs, [],
        4 * seq * model * units, seq * units,
    )


def closing(x0, eb, enc_gain, enc_sum, y0, sb, dec_gain, dec_sum, y2, last):
    seq, model = x0.shape
    inputs = [
        full(a) if a.shape[0] == 1 else (a, rows_spec(model))
        for a in (x0, eb, enc_gain, enc_sum, y0, sb, dec_gain, dec_sum, y2, last)
    ]
    return call(
        closing_kernel, "closing", (seq // ROWS,), inputs,
        row_outputs(seq, (model, F32), (model, F32), (model, BF16)), [], 20 * seq * model,
    )


def dot_rows(left, right):
    return lax.dot_general(
        left, right, (((0,), (0,)), ((), ())), preferred_element_type=jnp.float32
    )


def attention_weights_kernel(dq_ref, dk_ref, dv_ref, o_ref, n_ref, m_ref, g_ref, out_ref):
    count = dq_ref.shape[1]
    pairs = ((dq_ref, n_ref), (dk_ref, m_ref), (dv_ref, m_ref), (o_ref, g_ref))
    for i, (left, right) in enumerate(pairs):
        out_ref[i * count : (i + 1) * count, :] = dot_rows(left[...], right[...])


def attention_weights(grads, attended, normed, memory):
    seq, model = normed.shape
    width = attended.shape[1]
    inputs = [full(a) for a in (*grads[2:5], attended, normed, memory, grads[1])]
    outputs = [((4 * width, model), F32, whole((4 * width, model)))]
    return call(
        attention_weights_kernel, "attention_weights", (1,), inputs, outputs, [],
        8 * seq * model * width,
    )[0]


def attention_back(
    core, ql, kl, base, stream, dn, gain, wo, kept, wq, wk, wv, bias, x0, causal, name
):
    q, k, v, o, lse = kept
    seq, width = q.shape
    model = wo.shape[1]
    heads = width // DK
    biased = bias is not None
    inputs = [(core, SMEM_SPEC), (ql, SMEM_SPEC), (kl, SMEM_SPEC)]
    inputs += [(base, rows_spec(model)), (stream, rows_spec(model))]
    inputs += [(dn[0], rows_spec(model))] if len(dn) == 1 else [full(a) for a in dn]
    inputs += [full(gain), full(wo)]
    inputs += [(q, rows_spec(width)), full(k), full(v), (o, rows_spec(width)), (lse, lanes_spec())]
    inputs += [full(wq), full(wk), full(wv)]
    if biased:
        inputs += [full(bias[0]), full(bias[1]), full(x0)]
    outputs = [((seq, model), F32, rows_spec(model)), ((seq, model), BF16, rows_spec(model))]
    outputs += [((seq, width), BF16, whole((seq, width)))] * 3
    outputs.append(((1, model), F32, whole((1, model))))
    if biased:
        outputs.append((bias[1].shape, F32, whole(bias[1].shape)))
        outputs.append(((1, model), F32, whole((1, model))))
    outputs.append(((seq, model), F32, whole((seq, model))))
    if not biased:
        outputs.append(((seq, model), F32, whole((seq, model))))
    scratch = [
        pltpu.VMEM((width, seq), BF16),
        pltpu.VMEM((seq, TILE), jnp.int32),
        pltpu.VMEM((width, BQ), F32),
        pltpu.VMEM((seq, width), F32),
        pltpu.VMEM((seq, width), F32),
    ]
    if biased:
        scratch += [pltpu.VMEM((heads, 2 * seq - TILE, TILE), F32)] * 2
    result = call(
        functools.partial(attention_back_kernel, causal, biased, len(dn)),
        name, (seq // BQ,), inputs,
        outputs, scratch, 8 * seq * model * width + 5 * seq * seq * width, seq * seq,
    )
    return result[:6], result[6:]


MESH_ID = pl.DeviceIdType.MESH
MB_PER_ROW = 0.768 * 4 / 1000
RATES = (2.0, 21.0, 21.3, 21.5, 44.0)
DEPTH = 2


class Copies:
    def __init__(self, send_sem, recv_sem):
        self.send_sem, self.recv_sem = send_sem, recv_sem
        self.all, self.steps, self.first = [], [], []

    def copy(self, source, target, axis, index, link, rows, stage=0):
        i = len(self.all)

        def make():
            return pltpu.make_async_remote_copy(
                src_ref=source,
                dst_ref=target,
                send_sem=self.send_sem.at[i],
                recv_sem=self.recv_sem.at[i],
                device_id={axis: index},
                device_id_type=MESH_ID,
            )

        self.all.append((make, link, rows, stage))
        return i

    def step(self, waits, work, starts):
        self.steps.append((waits, work, starts))

    def start(self, i):
        make, link, rows, _ = self.all[i]
        self.made[i] = make()
        self.made[i].start()
        begin = max(self.now, self.free.get(link, 0.0))
        if link == 4:
            half = 22.0 * rows * MB_PER_ROW
            begin = max(begin, self.free.get(3, 0.0) - half)
            self.free[3] = max(self.free.get(3, 0.0), begin) + half
        self.free[link] = begin + RATES[link] * rows * MB_PER_ROW
        self.arrive[i] = self.free[link] + 1.0

    def fill(self):
        for i in sorted(self.pending, key=lambda i: (-self.all[i][3], i)):
            link = self.all[i][1]
            busy = sum(self.all[j][1] == link and self.arrive[j] > self.now for j in self.made)
            if busy < DEPTH or link < 2:
                self.pending.remove(i)
                self.start(i)

    def run(self):
        self.now, self.free, self.arrive, self.made = 0.0, {}, {}, {}
        self.pending = list(self.first)
        left = list(self.steps)
        self.fill()
        while left:
            ready = [s for s in left if all(i in self.made for i in s[0])]
            step = min(ready, key=lambda s: max([self.arrive[i] for i in s[0]], default=0.0))
            left.remove(step)
            for i in step[0]:
                self.made[i].wait_recv()
                self.now = max(self.now, self.arrive[i])
            if step[1] is not None:
                step[1]()
            self.pending += step[2]
            self.fill()
        for made in self.made.values():
            made.wait_send()


def mp_partners():
    me = lax.axis_index("mp")
    core = lax.rem(me, 2)
    return core, me + 1 - 2 * core, lax.rem(me + 2, 4)


def dp_side(bit):
    return lax.rem(lax.axis_index("dp") // (1 << bit), 2)


def dp_partner(bit):
    return lax.axis_index("dp") + (1 << bit) * (1 - 2 * dp_side(bit))


def greet(bits):
    barrier = pltpu.get_barrier_semaphore()
    _, beside, across = mp_partners()
    ids = [{"mp": beside}, {"mp": across}] + [{"dp": dp_partner(bit)} for bit in bits]
    for device_id in ids:
        pl.semaphore_signal(barrier, inc=1, device_id=device_id, device_id_type=MESH_ID)
    pl.semaphore_wait(barrier, len(ids))


def rows_at(start, count):
    return pl.ds(pl.multiple_of(start, 8), count)


def mp_job(copies, part_ref, near_ref, far_ref, out_ref, chunks, finish=None, far=True):
    core, beside, across = mp_partners()
    count = part_ref.shape[0] // (2 * chunks)

    def one(k):
        mine = rows_at((2 * k + core) * count, count)
        other = rows_at((2 * k + 1 - core) * count, count)
        first = copies.copy(part_ref.at[other, :], near_ref.at[k], "mp", beside, 0, count)
        copies.first.append(first)

        def add_near():
            near_ref[k] = part_ref[mine, :] + near_ref[k]

        second = copies.copy(near_ref.at[k], far_ref.at[k], "mp", across, 1, count)
        copies.step([first], add_near, [second])

        def add_far():
            out_ref[mine, :] = near_ref[k] + far_ref[k]
            if finish is not None:
                finish(mine)

        third = copies.copy(out_ref.at[mine, :], out_ref.at[mine, :], "mp", beside, 0, count)
        copies.step([second], add_far, [third])
        copies.step([third], None if finish is None else lambda: finish(other), [])

    for k in range(chunks):
        one(k)


def near_job(copies, part_ref, land_ref, out_ref):
    core, beside, _ = mp_partners()
    count = part_ref.shape[0] // 2
    mine = rows_at(core * count, count)
    other = rows_at((1 - core) * count, count)
    first = copies.copy(part_ref.at[other, :], land_ref, "mp", beside, 0, count)
    copies.first.append(first)

    def add():
        out_ref[...] = part_ref[mine, :] + land_ref[...]

    copies.step([first], add, [])


LINKS = (2, 3, 4)


def scatter_job(copies, part_ref, land_refs, bits, base, rows, store, got_ref=None):
    start, count, waits, work = base, rows, None, None
    source, origin = part_ref, 0
    for level, bit in enumerate(bits):
        count = count // 2
        side = dp_side(bit)
        keep = start + side * count
        give = start + (1 - side) * count
        land = land_refs[level]
        place = base // rows * count
        landing = slice(place, place + count)
        got = land
        if level == 0 and got_ref is not None:
            made, got = None, got_ref
        else:
            made = copies.copy(
                source.at[rows_at(give - origin, count), :], land.at[landing, :], "dp",
                dp_partner(bit), LINKS[min(bit, 2)], count, level,
            )
            if level == 0:
                copies.first.append(made)
            else:
                copies.step(waits, work, [made])

        def work(
            source=source, origin=origin, keep=keep, land=land, got=got, landing=landing, count=count
        ):
            land[landing, :] = source[rows_at(keep - origin, count), :] + got[landing, :]

        waits = [] if made is None else [made]
        source, origin, start = land, keep - place, keep

    def last(add=work, land=land, landing=landing, start=start, count=count):
        add()
        store(start, count, land[landing, :])

    return waits, last


def gather_job(copies, out_ref, bits, base, rows, waits, work):
    count = rows >> len(bits)
    start, size = base, rows
    for bit in bits:
        size = size // 2
        start = start + dp_side(bit) * size
    for level, bit in enumerate(reversed(bits)):
        held = rows_at(start, count)
        made = copies.copy(
            out_ref.at[held, :], out_ref.at[held, :], "dp", dp_partner(bit),
            LINKS[min(bit, 2)], count, len(bits) + level,
        )
        if waits is None:
            work()
            copies.first.append(made)
        else:
            copies.step(waits, work, [made])
        waits, work = [made], None
        start = start - dp_side(bit) * count
        count = count * 2
    copies.step(waits, None, [])


def small_job(copies, small_ref, land_ref, held_ref, out_ref, bits, shared):
    core, beside, across = mp_partners()
    hops = [("mp", beside, 0), ("mp", across, 1)]
    hops += [("dp", dp_partner(bit), LINKS[min(bit, 2)]) for bit in bits]
    count = small_ref.shape[0]
    first_rows = lax.broadcasted_iota(jnp.int32, small_ref.shape, 0) < shared
    source, waits, work = small_ref, None, None
    for i, (axis, index, link) in enumerate(hops):
        made = copies.copy(source, land_ref.at[i], axis, index, link, count)
        if i == 0:
            copies.first.append(made)
        else:
            copies.step(waits, work, [made])

        def work(i=i, source=source, last=i == len(hops) - 1):
            got = land_ref[i]
            if i < 2:
                got = jnp.where(first_rows, got, 0.0)
            target = out_ref if last else held_ref.at[i]
            target[...] = source[...] + got

        waits, source = [made], held_ref.at[i]
    copies.step(waits, work, [])


CHUNKS = 4
PIECES = 4


def sums(number, parts=(), near=(), scatter=(), gather=(), units=(), turns=(), halves=(), small=None, shared=0):
    bits = list(range((lax.axis_size("dp") - 1).bit_length()))
    turned = bits[1:] + bits[:1]
    dp = bool(scatter or gather or units or small is not None)
    smalls = [] if small is None else [small]
    inputs = [*parts, *near, *scatter, *gather, *units, *smalls, *halves]
    model = inputs[0].shape[1]
    shares = lax.axis_size("dp")
    outputs = [(a.shape, F32) for a in parts]
    outputs += [((a.shape[0] // 2, model), F32) for a in near]
    outputs += [((a.shape[0] // shares, model), F32) for a in scatter]
    outputs += [((a.shape[0] * shares, model), F32) for a in gather]
    outputs += [(a.shape, F32) for a in (*units, *smalls)]
    lands = []
    for a in parts:
        lands += [pltpu.VMEM((CHUNKS, a.shape[0] // (2 * CHUNKS), model), F32)] * 2
    for a in near:
        lands.append(pltpu.VMEM((a.shape[0] // 2, model), F32))
    for a in (*scatter, *units):
        lands += [pltpu.VMEM((a.shape[0] >> (i + 1), model), F32) for i in range(len(bits))]
    for a in smalls:
        lands += [pltpu.VMEM((2 + len(bits), *a.shape), F32)] * 2
    count, ends = len(inputs), len(inputs) + len(outputs)
    total = 3 * CHUNKS * len(parts) + len(near) + len(smalls) * (2 + len(bits))
    total += len(bits) * PIECES * (len(scatter) + len(gather) + 2 * len(units))

    def kernel(*refs):
        ins, outs = list(refs[:count]), list(refs[count:ends])
        scratch = list(refs[ends:-2])
        half_refs = [None] * (len(units) - len(halves)) + ins[count - len(halves) :]
        greet(bits if dp else [])
        copies = Copies(refs[-2], refs[-1])
        for _ in parts:
            mp_job(copies, ins.pop(0), scratch.pop(0), scratch.pop(0), outs.pop(0), CHUNKS)
        for _ in near:
            near_job(copies, ins.pop(0), scratch.pop(0), outs.pop(0))
        for a in scatter:
            part_ref, out_ref = ins.pop(0), outs.pop(0)
            land_refs = [scratch.pop(0) for _ in bits]
            rows = a.shape[0] // PIECES
            for piece in range(PIECES):

                def keep(start, count, value, piece=piece, out_ref=out_ref):
                    out_ref[piece * count : (piece + 1) * count, :] = value

                waits, work = scatter_job(
                    copies, part_ref, land_refs, bits, piece * rows, rows, keep
                )
                copies.step(waits, work, [])
        for a in gather:
            part_ref, out_ref = ins.pop(0), outs.pop(0)
            rows = a.shape[0] * shares // PIECES
            for piece in range(PIECES):
                start, size = piece * rows, rows
                for bit in bits:
                    size = size // 2
                    start = start + dp_side(bit) * size

                def put(start=start, size=size, piece=piece, part_ref=part_ref, out_ref=out_ref):
                    out_ref[rows_at(start, size), :] = part_ref[
                        piece * size : (piece + 1) * size, :
                    ]

                gather_job(copies, out_ref, bits, piece * rows, rows, None, put)
        for a, half_ref in zip(units, half_refs):
            part_ref, out_ref = ins.pop(0), outs.pop(0)
            land_refs = [scratch.pop(0) for _ in bits]
            rows = a.shape[0] // PIECES
            for piece in range(PIECES):

                def keep(start, count, value, out_ref=out_ref):
                    out_ref[rows_at(start, count), :] = value

                order = turned if piece in turns else bits
                waits, work = scatter_job(
                    copies, part_ref, land_refs, order, piece * rows, rows, keep, half_ref
                )
                gather_job(copies, out_ref, order, piece * rows, rows, waits, work)
        if small is not None:
            small_job(copies, ins[0], scratch[0], scratch[1], outs[0], bits, shared)
        copies.run()

    result = pl.pallas_call(
        kernel,
        in_specs=[whole(a.shape) for a in inputs],
        out_specs=[whole(shape) for shape, _ in outputs],
        out_shape=[jax.ShapeDtypeStruct(shape, dtype) for shape, dtype in outputs],
        grid=(1,),
        scratch_shapes=lands
        + [pltpu.SemaphoreType.DMA((total,)), pltpu.SemaphoreType.DMA((total,))],
        compiler_params=pltpu.CompilerParams(
            collective_id=number, has_side_effects=True, vmem_limit_bytes=VMEM_BYTES
        ),
        cost_estimate=pl.CostEstimate(flops=1, bytes_accessed=1, transcendentals=0),
        name="sums",
    )(*inputs)
    groups = []
    for group in (parts, near, scatter, gather, units, smalls):
        groups.append(list(result[: len(group)]))
        result = result[len(group) :]
    return groups


def first_half(unit):
    rows = unit.shape[0] // (2 * PIECES)
    pieces = unit.reshape(PIECES, 2, rows, unit.shape[1])
    other = 1 - lax.rem(lax.axis_index("dp"), 2)
    return lax.dynamic_index_in_dim(pieces, other, 1, False).reshape(PIECES * rows, -1)


def first_swap(value):
    pairs = [(i, i ^ 1) for i in range(lax.axis_size("dp"))]
    return lax.ppermute(value, "dp", pairs)


def shares_fit(rows):
    return rows % (8 * PIECES * lax.axis_size("dp")) == 0


CORE_SWAP = [(0, 1), (1, 0), (2, 3), (3, 2)]
CHIP_SWAP = [(0, 2), (2, 0), (1, 3), (3, 1)]


def core_swap(value):
    return lax.ppermute(value, "mp", CORE_SWAP)


def chip_swap(value):
    return lax.ppermute(value, "mp", CHIP_SWAP)


def part(value, start, rows):
    return lax.dynamic_slice_in_dim(value, start, rows, axis=0)


class Chain:
    def __init__(self):
        self.token = None

    def tie(self, value):
        if self.token is None:
            return value
        value, _ = lax.optimization_barrier((value, self.token))
        return value

    def mark(self, value):
        self.token = value


class Wire:
    def __init__(self, chain, swap):
        self.chain, self.swap = chain, swap

    def send(self, value):
        self.value = self.swap(self.chain.tie(value))

    def wait(self):
        self.value = self.chain.tie(self.value)
        self.chain.mark(self.value)
        return self.value


class Gather:
    def __init__(self, chain):
        self.chain = chain
        self.y, self.s, self.r = [Wire(chain, swap) for swap in (chip_swap, core_swap, core_swap)]

    def put(self, own):
        self.own = own

    def sy(self):
        self.y.send(self.own)

    def wy(self):
        self.y.wait()

    def ss(self):
        self.s.send(self.own)

    def ws(self):
        self.s.wait()

    def sr(self):
        self.r.send(self.y.value)

    def wr(self):
        self.r.wait()

    def pieces(self):
        return (self.own, self.y.value, self.s.value, self.r.value)


def project_weight(left, right):
    return lax.dot_general(
        left, right, (((0,), (0,)), ((), ())), preferred_element_type=jnp.float32
    )


def signed_buckets(buckets, seq):
    fill = jnp.full((2 * seq - buckets.shape[0],), -1, jnp.int32)
    return jnp.concatenate([fill, buckets])[None, :]


def body(
    encoder_input,
    decoder_input,
    encoder_lengths,
    decoder_lengths,
    encoder_buckets,
    decoder_buckets,
    encoder_attn_gain,
    encoder_query,
    encoder_key,
    encoder_value,
    encoder_output,
    encoder_bias,
    encoder_ffn_gain,
    encoder_ffn_in,
    encoder_ffn_out,
    decoder_attn_gain,
    decoder_query,
    decoder_key,
    decoder_value,
    decoder_output,
    decoder_bias,
    cross_gain,
    cross_query,
    cross_key,
    cross_value,
    cross_output,
    decoder_ffn_gain,
    decoder_ffn_in,
    decoder_ffn_out,
    encoder_cotangent,
    decoder_cotangent,
):
    _, seq, width = encoder_input.shape
    enc_lens, dec_lens = encoder_lengths, decoder_lengths
    enc_bias = (signed_buckets(encoder_buckets, seq), encoder_bias)
    dec_bias = (signed_buckets(decoder_buckets, seq), decoder_bias)
    me = lax.axis_index("mp").astype(jnp.int32).reshape(1)
    core = lax.rem(me, 2)
    x0, y0 = encoder_input[0], decoder_input[0]
    enc_cot, dec_cot = encoder_cotangent[0], decoder_cotangent[0]
    row = lambda gain: gain[None, :]
    encoder_query, encoder_key, encoder_value = encoder_query.T, encoder_key.T, encoder_value.T
    decoder_query, decoder_key, decoder_value = decoder_query.T, decoder_key.T, decoder_value.T
    cross_query, cross_key, cross_value = cross_query.T, cross_key.T, cross_value.T
    chain = Chain()
    tie, mark = chain.tie, chain.mark

    wide_e, wide, e, d, x = [Gather(chain) for _ in range(5)]
    wide_e.put(encoder_output.astype(F32))
    mark(wide_e.own)
    wide_e.sy()
    count = encoder_output.shape[0] // lax.axis_size("dp")
    place = lax.axis_index("dp") * count
    slices = Wire(chain, chip_swap)
    slices.send(
        jnp.concatenate(
            [part(decoder_output, place, count), part(cross_output, place, count)], axis=1
        ).astype(F32)
    )
    enc, out = self_forward(
        enc_lens, tie(x0), row(encoder_attn_gain), encoder_query, encoder_key, encoder_value,
        enc_bias, False, "encoder_attention",
    )
    mark(out)
    e.put(out)
    wide_e.wy()
    slices.wait()
    e.sy()
    e.ss()
    wide.y.value = lax.all_gather(tie(slices.value), "dp", axis=0, tiled=True)
    wide_e.sr()
    wide_e.ss()

    dec, out = self_forward(
        dec_lens, tie(y0), row(decoder_attn_gain), decoder_query, decoder_key, decoder_value,
        dec_bias, True, "decoder_attention",
    )
    mark(out)
    d.put(out)
    e.wy()
    e.sr()
    d.sy()
    e.ws()
    wide_e.ws()
    wide_e.wr()
    e.wr()
    own = jnp.concatenate([decoder_output, cross_output], axis=1).astype(F32)
    wide.put(own)

    ffn = ffn_forward(
        me, tie(x0), e.pieces(), wide_e.pieces(), row(encoder_ffn_gain), encoder_ffn_in,
        encoder_ffn_out,
    )
    mark(ffn[4])
    d.wy()
    d.ss()
    d.sr()
    wide.ss()
    enc_sum = sums(1, parts=[tie(ffn[4])])[0][0]
    mark(enc_sum)
    wide.sr()
    d.ws()
    d.wr()
    wide.ws()
    wide.wr()

    split = lambda i: tuple(value[:, i * width : (i + 1) * width] for value in wide.pieces())
    cross, out = cross_forward(
        me, dec_lens, enc_lens, tie(y0), d.pieces(), split(0), ffn[0], enc_sum, row(cross_gain),
        cross_query, cross_key, cross_value,
    )
    mark(out)
    x.put(out)
    x.sy()
    x.ss()
    x.wy()
    x.sr()
    x.ws()
    x.wr()

    both = ffn_both(
        me, tie(cross[0]), x.pieces(), split(1), row(decoder_ffn_gain), decoder_ffn_in,
        decoder_ffn_out, dec_cot,
    )
    mark(both[4])
    dec_ffn = jnp.concatenate(
        [project_weight(tie(both[1]), both[3]), project_weight(both[2], dec_cot)], axis=0
    )
    mark(dec_ffn)
    dec_ffn = lax.psum(dec_ffn, "dp")
    dn = sums(2, parts=[tie(both[4])])[0][0]
    mark(dn)

    cb, (own_part, memory_part) = attention_back(
        core, dec_lens, enc_lens, dec_cot, both[0], (tie(dn),), row(decoder_ffn_gain),
        cross_output, cross[3:8], cross_query, cross_key, cross_value, None, None, False,
        "cross_back",
    )
    mark(own_part)
    unit_2 = attention_weights((*cb[:2], tie(cb[2]), *cb[3:]), cross[6], cross[1], cross[2])
    mark(unit_2)
    split_units = shares_fit(width)
    totals, nears, shares, _, _, _ = sums(
        3, parts=[tie(memory_part)], near=[own_part], scatter=[unit_2] if split_units else []
    )
    grad_memory, own_near = totals[0], nears[0]
    mark(grad_memory)

    back = ffn_backward(enc_cot, tie(grad_memory), ffn[2], encoder_ffn_in, encoder_ffn_out)
    mark(back[3])
    unit_4a = project_weight(tie(ffn[1]), back[2])
    mark(unit_4a)
    unit_4b = project_weight(tie(ffn[3]), back[1])
    mark(unit_4b)
    totals, _, shares, wholes, _, _ = sums(
        4, parts=[tie(back[3])], scatter=[unit_4a] if split_units else [], gather=shares
    )
    dn = totals[0]
    mark(dn)
    half_4b, half_5 = [Wire(chain, first_swap) for _ in range(2)]
    half_4b.send(first_half(unit_4b))
    own_far, own_beside, own_relay = [
        Wire(chain, swap) for swap in (chip_swap, core_swap, core_swap)
    ]
    own_far.send(own_near)
    own_beside.send(own_near)

    eb, (enc_table, enc_gain, enc_part) = attention_back(
        core, enc_lens, enc_lens, back[0], ffn[0], (tie(dn),), row(encoder_ffn_gain),
        encoder_output, enc[1:6], encoder_query, encoder_key, encoder_value, enc_bias, x0, False,
        "encoder_back",
    )
    mark(enc_part)
    own_beside.wait()
    own_far.wait()
    own_relay.send(own_far.value)
    half_4b.wait()
    dec_ffn = tie(dec_ffn)
    mark(dec_ffn)
    unit_5 = attention_weights((*eb[:2], tie(eb[2]), *eb[3:]), enc[4], enc[0], enc[0])
    mark(unit_5)
    half_5.send(first_half(unit_5))
    own_relay.wait()

    own_pieces = (own_near, own_far.value, own_beside.value, own_relay.value)
    sb, (dec_table, dec_gain, dec_part) = attention_back(
        core, dec_lens, dec_lens, tie(cb[0]), cross[0], own_pieces, row(cross_gain),
        decoder_output, dec[1:6], decoder_query, decoder_key, decoder_value, dec_bias, y0, True,
        "decoder_back",
    )
    mark(dec_part)
    half_5.wait()
    unit_3 = attention_weights(sb, dec[4], dec[0], dec[0])
    tables = []
    for table in (enc_table, dec_table):
        flat = table.reshape(1, -1)
        tables.append(jnp.pad(flat, ((0, 0), (0, width - flat.shape[1]))))
    blank = jnp.zeros((1, width), F32)
    small = jnp.concatenate([enc_gain, dec_gain, eb[5], sb[5], cb[5], *tables, blank], axis=0)
    units = [unit_3, unit_4b, unit_5] if split_units else []
    halves = [half_4b.value, half_5.value] if split_units else []
    totals, _, _, gathered, units, smalls = sums(
        5, parts=[enc_part, dec_part, both[5]], gather=shares, units=units, halves=halves,
        small=small, shared=2
    )
    small = smalls[0]
    if split_units:
        unit_2, unit_4a = wholes[0], gathered[0]
        unit_3, unit_4b, unit_5 = units
    else:
        unit_2, unit_4a, unit_3, unit_4b, unit_5 = lax.psum(
            (unit_2, unit_4a, unit_3, unit_4b, unit_5), "dp"
        )
    enc_grad, dec_grad, result = closing(
        x0, eb[0], row(encoder_attn_gain), totals[0], y0, sb[0], row(decoder_attn_gain), totals[1],
        both[0], totals[2],
    )

    def matrices(stack):
        count = stack.shape[0] // 4
        pieces = [stack[i * count : (i + 1) * count] for i in range(4)]
        return [jnp.transpose(piece) for piece in pieces[:3]] + pieces[3:]

    shape = encoder_bias.shape
    count = shape[0] * shape[1]
    return (
        cross[2][None],
        result[None],
        enc_grad[None],
        dec_grad[None],
        small[0],
        *matrices(unit_5),
        small[5, :count].reshape(shape),
        small[2],
        unit_4a,
        unit_4b,
        small[1],
        *matrices(unit_3),
        small[6, :count].reshape(shape),
        small[3],
        *matrices(unit_2),
        small[4],
        dec_ffn[:width],
        dec_ffn[width:],
    )


def solution(mesh):
    return jax.shard_map(
        body,
        mesh=mesh,
        in_specs=(
            P("dp", None, None),
            P("dp", None, None),
            P("dp", None),
            P("dp", None),
            P(),
            P(),
            P(),
            P(None, "mp"),
            P(None, "mp"),
            P(None, "mp"),
            P("mp", None),
            P(None, "mp"),
            P(),
            P(None, "mp"),
            P("mp", None),
            P(),
            P(None, "mp"),
            P(None, "mp"),
            P(None, "mp"),
            P("mp", None),
            P(None, "mp"),
            P(),
            P(None, "mp"),
            P(None, "mp"),
            P(None, "mp"),
            P("mp", None),
            P(),
            P(None, "mp"),
            P("mp", None),
            P("dp", None, None),
            P("dp", None, None),
        ),
        out_specs=(
            P("dp", None, None),
            P("dp", None, None),
            P("dp", None, None),
            P("dp", None, None),
            P(),
            P(None, "mp"),
            P(None, "mp"),
            P(None, "mp"),
            P("mp", None),
            P(None, "mp"),
            P(),
            P(None, "mp"),
            P("mp", None),
            P(),
            P(None, "mp"),
            P(None, "mp"),
            P(None, "mp"),
            P("mp", None),
            P(None, "mp"),
            P(),
            P(None, "mp"),
            P(None, "mp"),
            P(None, "mp"),
            P("mp", None),
            P(),
            P(None, "mp"),
            P("mp", None),
        ),
        check_vma=False,
    )
```

```python
import functools

import jax
import jax.numpy as jnp
from jax import lax
from jax.experimental import pallas as pl
from jax.experimental.pallas import tpu as pltpu
from jax.sharding import PartitionSpec as P

DK = 64
EPS = 1e-06
NEG = -1e30
HIGHEST = lax.Precision.HIGHEST
TILE = 128
BQ = 256
KC = 256
SPEEDUP = 1 << 20
VMEM_BYTES = 60 * 1024 * 1024


def doc_ends(lens_ref):
    ends = []
    total = jnp.int32(0)
    for j in range(lens_ref.shape[1]):
        total = total + lens_ref[0, j]
        ends.append(total)
    return ends


def docs_at(places, ends):
    result = jnp.zeros(places.shape, jnp.int32)
    for end in ends:
        result = result + (places >= end).astype(jnp.int32)
    return result


def key_range(ql_ref, q_ends, kl_ref, block, causal):
    first = block * BQ
    last = first + BQ - 1
    low = jnp.int32(0)
    high = jnp.int32(0)
    for j, end in enumerate(q_ends):
        low = low + jnp.where(end <= first, kl_ref[0, j], 0)
        high = high + jnp.where(end - ql_ref[0, j] <= last, kl_ref[0, j], 0)
    if causal:
        high = jnp.minimum(high, first + BQ)
    return low // KC, (high + KC - 1) // KC


def bucket_hits(buckets_ref, count):
    ids = lax.broadcasted_iota(jnp.int32, (count, buckets_ref.shape[1]), 0)
    return ids == buckets_ref[...]


def make_tiles(buckets_ref, table_ref, tiles_ref):
    hits = bucket_hits(buckets_ref, table_ref.shape[0])
    width = buckets_ref.shape[1]
    for h in range(tiles_ref.shape[0]):
        row = jnp.sum(jnp.where(hits, table_ref[:, h : h + 1], 0.0), axis=0, keepdims=True)
        row = jnp.where(buckets_ref[...] < 0, NEG, row)
        for k in range(tiles_ref.shape[1] // TILE):
            start = width - 2 * TILE - k * TILE
            window = jnp.broadcast_to(row[:, start : start + 2 * TILE], (TILE, 2 * TILE))
            skewed = pltpu.roll(window, 0, 1, stride=1, stride_axis=0)
            tiles_ref[h, k * TILE : (k + 1) * TILE, :] = skewed[:, TILE:]


def sum_tiles(buckets_ref, grad_tiles_ref, grad_table_ref):
    count = grad_table_ref.shape[0]
    width = buckets_ref.shape[1]
    hits = bucket_hits(buckets_ref, count)
    blocks = grad_tiles_ref.shape[1] // TILE
    blank = jnp.zeros((8, TILE), jnp.float32)
    for h in range(grad_tiles_ref.shape[0]):
        halves = []
        for k in range(blocks):
            total = jnp.zeros((8, 2 * TILE), jnp.float32)
            for a in range(0, TILE, 8):
                piece = grad_tiles_ref[h, k * TILE + a : k * TILE + a + 8, :]
                wide = jnp.concatenate([blank, piece], axis=1)
                total = total + pltpu.roll(wide, (2 * TILE - a) % (2 * TILE), 1)
            halves.append(total)
        parts = []
        for m in range(width // TILE):
            upper = halves[blocks - 1 - m][:, :TILE] if m < blocks else None
            lower = halves[blocks - m][:, TILE:] if m >= 1 else None
            part = upper if lower is None else lower if upper is None else upper + lower
            parts.append(part)
        group = jnp.concatenate(parts, axis=1)
        row = group[0:1]
        for b in range(1, 8):
            row = row + pltpu.roll(group[b : b + 1], width - b, 1)
        grad_table_ref[:, h : h + 1] = jnp.sum(jnp.where(hits, row, 0.0), axis=1, keepdims=True)


def tile_rows(tiles_ref, h, block, chunk, keys):
    parts = []
    for t in range(BQ // TILE):
        start = keys - TILE - TILE * (block * (BQ // TILE) + t) + chunk * KC
        parts.append(tiles_ref[h, pl.ds(pl.multiple_of(start, TILE), KC), :])
    return jnp.concatenate(parts, axis=1)


def head_mask(h, width):
    lane = lax.broadcasted_iota(jnp.int32, (1, width), 1)
    return ((lane >= h * DK) & (lane < (h + 1) * DK)).astype(jnp.bfloat16)


def dot_last(left, right):
    return lax.dot_general(
        left, right, (((1,), (1,)), ((), ())), preferred_element_type=jnp.float32
    )


def dot(left, right):
    return jnp.dot(left, right, preferred_element_type=jnp.float32)


def flip(value):
    return jnp.transpose(value.astype(jnp.float32)).astype(value.dtype)


ROWS = 256


def ref_norm(stream, gain):
    scale = lax.rsqrt(jnp.mean(stream * stream, axis=-1, keepdims=True) + EPS)
    return stream * scale * gain


def norm_back(stream, gain, grad_normed):
    scale = lax.rsqrt(jnp.mean(stream * stream, axis=-1, keepdims=True) + EPS)
    unit = stream * scale
    scaled = gain * grad_normed
    grad = scale * (scaled - unit * jnp.mean(scaled * unit, axis=-1, keepdims=True))
    return grad, jnp.sum(grad_normed * unit, axis=0, keepdims=True)


GELU_SCALE = 0.7978845608028654
GELU_CUBE = 0.044715


def gelu_parts(value):
    square = value * value
    curve = jnp.tanh(GELU_SCALE * (value + GELU_CUBE * value * square))
    active = 0.5 * value * (1.0 + curve)
    slope = 0.5 * (1.0 + curve) + 0.5 * value * (1.0 - curve * curve) * GELU_SCALE * (
        1.0 + 3.0 * GELU_CUBE * square
    )
    return active, slope


def block_rows(index):
    return pl.ds(pl.multiple_of(index * ROWS, ROWS), ROWS)


def attend_block(block, causal, biased, ql_ref, kl_ref, q_block, k_ref, vt_ref, kd_ref, s_ref, o_acc, tiles_ref, lse_ref):
    keys, width = k_ref.shape
    heads = width // DK
    q_ends = doc_ends(ql_ref)
    q_docs = docs_at(block * BQ + lax.broadcasted_iota(jnp.int32, (1, BQ), 1), q_ends)
    queries = q_block * jnp.bfloat16(DK ** (-0.5))
    masked = [queries * head_mask(h, width) for h in range(heads)]
    low, high = key_range(ql_ref, q_ends, kl_ref, block, causal)

    def first(chunk, tops):
        rows = pl.ds(pl.multiple_of(chunk * KC, KC), KC)
        docs = jnp.concatenate([kd_ref[rows, :]] * (BQ // TILE), axis=1)
        allowed = docs == q_docs
        fresh = []
        for h in range(heads):
            scores = dot_last(k_ref[rows, :], masked[h])
            if biased:
                scores = scores + tile_rows(tiles_ref, h, block, chunk, keys)
            scores = jnp.where(allowed, scores, NEG)
            s_ref[h, rows, :] = scores
            fresh.append(jnp.maximum(tops[h], jnp.max(scores, axis=0, keepdims=True)))
        return tuple(fresh)

    tops = lax.fori_loop(
        low, high, first, tuple(jnp.full((1, BQ), NEG, jnp.float32) for _ in range(heads))
    )
    o_acc[...] = jnp.zeros_like(o_acc)

    def second(chunk, totals):
        rows = pl.ds(pl.multiple_of(chunk * KC, KC), KC)
        fresh = []
        for h in range(heads):
            probs = jnp.exp(s_ref[h, rows, :] - tops[h])
            fresh.append(totals[h] + jnp.sum(probs, axis=0, keepdims=True))
            o_acc[h * DK : (h + 1) * DK, :] += dot(
                vt_ref[h * DK : (h + 1) * DK, rows], probs.astype(jnp.bfloat16)
            )
        return tuple(fresh)

    totals = lax.fori_loop(
        low, high, second, tuple(jnp.zeros((1, BQ), jnp.float32) for _ in range(heads))
    )
    outs = []
    for h in range(heads):
        lse_ref[h : h + 1, :] = tops[h] + jnp.log(totals[h])
        outs.append(o_acc[h * DK : (h + 1) * DK, :] / totals[h])
    return jnp.concatenate(outs, axis=0).astype(jnp.bfloat16).astype(jnp.float32)


def put_out(out, o_ref, ot_ref):
    o_ref[...] = jnp.transpose(out).astype(jnp.bfloat16)
    ot_ref[...] = out


def order_pieces(me, own, far, sib, sibfar, target_ref):
    other = lax.rem(me + 2, 4)
    beside = me + 1 - 2 * lax.rem(me, 2)
    target_ref[me] = own
    target_ref[other] = far
    target_ref[beside] = sib
    target_ref[lax.rem(beside + 2, 4)] = sibfar


def order_weights(me, refs, target_ref):
    order_pieces(me, *[ref[...].astype(jnp.bfloat16) for ref in refs], target_ref)


def out_product(me, refs, lanes, weights_ref, pieces_ref):
    order_pieces(me, *[ref[:, lanes] for ref in refs], pieces_ref)
    total = None
    for m in range(4):
        left = jnp.transpose(pieces_ref[m]).astype(jnp.bfloat16)
        product = dot(left, weights_ref[m])
        total = product if total is None else total + product
    return total


def self_forward_kernel(causal, *refs):
    ql_ref, x_ref, gain_ref, wq_ref, wk_ref, wv_ref, buckets_ref, table_ref = refs[:8]
    n_ref, q_ref, k_ref, v_ref, o_ref, lse_ref = refs[8:14]
    ot_ref = refs[14]
    vt_ref, kd_ref, s_ref, o_acc, tiles_ref = refs[15:]
    block = pl.program_id(0)
    keys = k_ref.shape[0]

    @pl.when(block == 0)
    def _():
        for b in range(keys // ROWS):
            rows = slice(b * ROWS, (b + 1) * ROWS)
            normed = ref_norm(x_ref[rows, :].astype(jnp.float32), gain_ref[...]).astype(
                jnp.bfloat16
            )
            n_ref[rows, :] = normed
            q_ref[rows, :] = dot_last(normed, wq_ref[...]).astype(jnp.bfloat16)
            k_ref[rows, :] = dot_last(normed, wk_ref[...]).astype(jnp.bfloat16)
            value = dot_last(normed, wv_ref[...])
            v_ref[rows, :] = value.astype(jnp.bfloat16)
            vt_ref[:, rows] = jnp.transpose(value).astype(jnp.bfloat16)
        kd_ref[...] = docs_at(
            lax.broadcasted_iota(jnp.int32, (keys, TILE), 0), doc_ends(ql_ref)
        )
        make_tiles(buckets_ref, table_ref, tiles_ref)

    out = attend_block(
        block, causal, True, ql_ref, ql_ref, q_ref[block_rows(block), :],
        k_ref, vt_ref, kd_ref, s_ref, o_acc, tiles_ref, lse_ref,
    )
    put_out(out, o_ref, ot_ref)


def cross_forward_kernel(*refs):
    me_ref, ql_ref, kl_ref, y0_ref = refs[:4]
    dec_pieces, dec_weights = refs[4:8], refs[8:12]
    x1_ref, enc_sum_ref, gain_ref, wq_ref, wk_ref, wv_ref = refs[12:18]
    y1_ref, n_ref, memory_ref, q_ref, k_ref, v_ref, o_ref, lse_ref, ot_ref = refs[18:27]
    vt_ref, kd_ref, s_ref, o_acc, weights_ref, pieces_ref = refs[27:]
    block = pl.program_id(0)
    keys = k_ref.shape[0]
    me = me_ref[0]

    @pl.when(block == 0)
    def _():
        for b in range(keys // ROWS):
            rows = slice(b * ROWS, (b + 1) * ROWS)
            memory = (x1_ref[rows, :] + enc_sum_ref[rows, :]).astype(jnp.bfloat16)
            memory_ref[rows, :] = memory
            k_ref[rows, :] = dot_last(memory, wk_ref[...]).astype(jnp.bfloat16)
            value = dot_last(memory, wv_ref[...])
            v_ref[rows, :] = value.astype(jnp.bfloat16)
            vt_ref[:, rows] = jnp.transpose(value).astype(jnp.bfloat16)
        kd_ref[...] = docs_at(
            lax.broadcasted_iota(jnp.int32, (keys, TILE), 0), doc_ends(kl_ref)
        )
        order_weights(me, dec_weights, weights_ref)

    summed = out_product(me, dec_pieces, slice(None), weights_ref, pieces_ref)
    stream = y0_ref[...].astype(jnp.float32) + summed
    y1_ref[...] = stream
    normed = ref_norm(stream, gain_ref[...]).astype(jnp.bfloat16)
    n_ref[...] = normed
    queries = dot_last(normed, wq_ref[...]).astype(jnp.bfloat16)
    q_ref[...] = queries
    out = attend_block(
        block, False, False, ql_ref, kl_ref, queries,
        k_ref, vt_ref, kd_ref, s_ref, o_acc, None, lse_ref,
    )
    put_out(out, o_ref, ot_ref)


def ffn_forward_kernel(*refs):
    me_ref, x_ref = refs[:2]
    pieces, weights = refs[2:6], refs[6:10]
    gain_ref, wi_ref, wo_ref, x1_ref, n_ref, hid_ref, act_ref, part_ref = refs[10:18]
    weights_ref, pieces_ref = refs[18:]
    me = me_ref[0]

    @pl.when(pl.program_id(0) == 0)
    def _():
        order_weights(me, weights, weights_ref)

    summed = out_product(me, pieces, slice(None), weights_ref, pieces_ref)
    stream = x_ref[...].astype(jnp.float32) + summed
    x1_ref[...] = stream
    normed = ref_norm(stream, gain_ref[...]).astype(jnp.bfloat16)
    n_ref[...] = normed
    hidden = dot(normed, wi_ref[...])
    hid_ref[...] = hidden
    active = gelu_parts(hidden)[0].astype(jnp.bfloat16)
    act_ref[...] = active
    part_ref[...] = dot(active, wo_ref[...])


def ffn_both_kernel(*refs):
    me_ref, y_ref = refs[:2]
    pieces, weights = refs[2:6], refs[6:10]
    gain_ref, wi_ref, wo_ref, cot_ref = refs[10:14]
    y2_ref, n_ref, act_ref, dhid_ref, part_ref, out_part_ref, weights_ref, pieces_ref = refs[14:]
    me = me_ref[0]

    @pl.when(pl.program_id(0) == 0)
    def _():
        order_weights(me, weights, weights_ref)

    summed = out_product(me, pieces, slice(None), weights_ref, pieces_ref)
    stream = y_ref[...] + summed
    y2_ref[...] = stream
    normed = ref_norm(stream, gain_ref[...]).astype(jnp.bfloat16)
    n_ref[...] = normed
    active, slope = gelu_parts(dot(normed, wi_ref[...]))
    active = active.astype(jnp.bfloat16)
    act_ref[...] = active
    grad = (slope * dot_last(cot_ref[...], wo_ref[...])).astype(jnp.bfloat16)
    dhid_ref[...] = grad
    part_ref[...] = dot_last(grad, wi_ref[...])
    out_part_ref[...] = dot(active, wo_ref[...])


def ffn_backward_kernel(cot_ref, sum_ref, hid_ref, wi_ref, wo_ref, x_ref, g_ref, dhid_ref, part_ref):
    stream = cot_ref[...].astype(jnp.float32) + sum_ref[...]
    x_ref[...] = stream
    branch = stream.astype(jnp.bfloat16)
    g_ref[...] = branch
    slope = gelu_parts(hid_ref[...])[1]
    grad = (slope * dot_last(branch, wo_ref[...])).astype(jnp.bfloat16)
    dhid_ref[...] = grad
    part_ref[...] = dot_last(grad, wi_ref[...])


def half_rows(core, block, mine_ref, sib_ref):
    local = block_rows(lax.rem(block, 2))
    return jnp.where(block // 2 == core, mine_ref[local, :], sib_ref[local, :])


def piece_rows(core, block, refs):
    near, far, near_sib, far_sib = refs
    return half_rows(core, block, near, near_sib) + half_rows(core, block, far, far_sib)


def closing_kernel(x0_ref, eb_ref, egain_ref, z_ref, y0_ref, sb_ref, dgain_ref, s_ref, y2_ref, l_ref,
                   enc_ref, dec_ref, result_ref):
    for start, stream, gain, summed, out in (
        (x0_ref, eb_ref, egain_ref, z_ref, enc_ref), (y0_ref, sb_ref, dgain_ref, s_ref, dec_ref)
    ):
        grad, _ = norm_back(start[...].astype(jnp.float32), gain[...], summed[...])
        out[...] = stream[...] + grad
    result_ref[...] = (y2_ref[...] + l_ref[...]).astype(result_ref.dtype)


def attention_back_kernel(causal, biased, pieces, *refs):
    refs = list(refs)
    take = lambda n: [refs.pop(0) for _ in range(n)]
    core_ref, ql_ref, kl_ref = take(3)
    base_ref, stream_ref = take(2)
    dn_refs = take(pieces)
    gain_ref, wo_ref, q_ref, k_ref, v_ref, o_ref, lse_ref, wq_ref, wk_ref, wv_ref = take(10)
    buckets_ref, table_ref, x0_ref = take(3) if biased else (None, None, None)
    x_ref, g_ref, dq_ref, dk_ref, dv_ref, gain_grad_ref = take(6)
    if biased:
        dtable_ref, own_gain_ref = take(2)
    part_ref = take(1)[0]
    memory_part_ref = None if biased else take(1)[0]
    kt_ref, kd_ref, dq_acc, dk_acc, dv_acc = take(5)
    tiles_ref, grad_ref = take(2) if biased else (None, None)
    block = pl.program_id(0)
    keys, width = k_ref.shape
    heads = width // DK
    core = core_ref[0]
    q_ends = doc_ends(ql_ref)
    scale = jnp.bfloat16(DK ** (-0.5))

    @pl.when(block == 0)
    def _():
        kt_ref[...] = flip(k_ref[...])
        kd_ref[...] = docs_at(
            lax.broadcasted_iota(jnp.int32, (keys, TILE), 0), doc_ends(kl_ref)
        )
        dk_acc[...] = jnp.zeros_like(dk_acc)
        dv_acc[...] = jnp.zeros_like(dv_acc)
        gain_grad_ref[...] = jnp.zeros_like(gain_grad_ref)
        if biased:
            make_tiles(buckets_ref, table_ref, tiles_ref)
            grad_ref[...] = jnp.zeros_like(grad_ref)

    if pieces == 1:
        grad_normed = dn_refs[0][...]
    else:
        grad_normed = piece_rows(core, block, dn_refs)
    grad_in, gain_grad = norm_back(stream_ref[...], gain_ref[...], grad_normed)
    gain_grad_ref[...] += gain_grad
    grad_stream = base_ref[...].astype(jnp.float32) + grad_in
    x_ref[...] = grad_stream
    branch = grad_stream.astype(jnp.bfloat16)
    g_ref[...] = branch
    grads = dot_last(branch, wo_ref[...]).astype(jnp.bfloat16)

    q_docs = docs_at(block * BQ + lax.broadcasted_iota(jnp.int32, (1, BQ), 1), q_ends)
    queries = q_ref[...] * scale
    product = grads.astype(jnp.float32) * o_ref[...].astype(jnp.float32)
    pick = jnp.concatenate(
        [head_mask(h, width).astype(jnp.float32) for h in range(heads)]
        + [jnp.zeros((8 - heads, width), jnp.float32)],
        axis=0,
    )
    inner = lax.dot_general(
        pick,
        product,
        (((1,), (1,)), ((), ())),
        precision=HIGHEST,
        preferred_element_type=jnp.float32,
    )
    q_masked = [queries * head_mask(h, width) for h in range(heads)]
    g_masked = [grads * head_mask(h, width) for h in range(heads)]
    low, high = key_range(ql_ref, q_ends, kl_ref, block, causal)
    dq_acc[...] = jnp.zeros_like(dq_acc)

    @pl.loop(low, high)
    def _(chunk):
        rows = pl.ds(pl.multiple_of(chunk * KC, KC), KC)
        docs = jnp.concatenate([kd_ref[rows, :]] * (BQ // TILE), axis=1)
        allowed = docs == q_docs
        dk = dk_acc[rows, :]
        dv = dv_acc[rows, :]
        for h in range(heads):
            scores = dot_last(k_ref[rows, :], q_masked[h])
            if biased:
                scores = scores + tile_rows(tiles_ref, h, block, chunk, keys)
            scores = jnp.where(allowed, scores, NEG)
            probs = jnp.exp(scores - lse_ref[h : h + 1, :])
            grad_probs = dot_last(v_ref[rows, :], g_masked[h])
            grad_scores = (probs * (grad_probs - inner[h : h + 1, :])).astype(jnp.bfloat16)
            dv = dv + dot(probs.astype(jnp.bfloat16), g_masked[h])
            dk = dk + dot(grad_scores, q_masked[h])
            dq_acc[h * DK : (h + 1) * DK, :] += dot(
                kt_ref[h * DK : (h + 1) * DK, rows], grad_scores
            )
            if biased:
                for t in range(BQ // TILE):
                    start = keys - TILE - TILE * (block * (BQ // TILE) + t) + chunk * KC
                    piece = pl.ds(pl.multiple_of(start, TILE), KC)
                    grad_ref[h, piece, :] += grad_scores[:, t * TILE : (t + 1) * TILE].astype(
                        jnp.float32
                    )
        dk_acc[rows, :] = dk
        dv_acc[rows, :] = dv

    dq = (jnp.transpose(dq_acc[...]) * DK ** (-0.5)).astype(jnp.bfloat16)
    dq_ref[block_rows(block), :] = dq

    @pl.when(block == pl.num_programs(0) - 1)
    def _():
        dk_ref[...] = dk_acc[...].astype(jnp.bfloat16)
        dv_ref[...] = dv_acc[...].astype(jnp.bfloat16)
        own_gain = jnp.zeros(gain_grad_ref.shape, jnp.float32)
        for b in range(keys // ROWS):
            rows = slice(b * ROWS, (b + 1) * ROWS)
            from_q = dot(dq_ref[rows, :], wq_ref[...])
            from_kv = dot(dk_ref[rows, :], wk_ref[...]) + dot(
                dv_ref[rows, :], wv_ref[...]
            )
            if not biased:
                part_ref[rows, :] = from_q
                memory_part_ref[rows, :] = from_kv
                continue
            total = from_q + from_kv
            part_ref[rows, :] = total
            start = x0_ref[rows, :].astype(jnp.float32)
            unit = start * lax.rsqrt(jnp.mean(start * start, axis=-1, keepdims=True) + EPS)
            own_gain = own_gain + jnp.sum(total * unit, axis=0, keepdims=True)
        if biased:
            own_gain_ref[...] = own_gain
            sum_tiles(buckets_ref, grad_ref, dtable_ref)


def whole(shape):
    return pl.BlockSpec(shape, lambda *_: (0,) * len(shape), pipeline_mode=pl.Buffered(1))


def rows_spec(width):
    return pl.BlockSpec((BQ, width), lambda i: (i, 0))


def lanes_spec():
    return pl.BlockSpec((8, BQ), lambda i: (0, i))


SMEM_SPEC = pl.BlockSpec(memory_space=pltpu.SMEM)
BF16, F32 = jnp.bfloat16, jnp.float32


def call(kernel, name, grid, inputs, outputs, scratch, flops, exps=0):
    def size(shape, dtype):
        count = 1
        for dim in shape:
            count *= dim
        return count * jnp.dtype(dtype).itemsize

    moved = sum(size(a.shape, a.dtype) for a, _ in inputs) + sum(size(s, d) for s, d, _ in outputs)
    return pl.pallas_call(
        kernel,
        grid=grid,
        in_specs=[spec for _, spec in inputs],
        out_specs=[spec for _, _, spec in outputs],
        out_shape=[jax.ShapeDtypeStruct(shape, dtype) for shape, dtype, _ in outputs],
        scratch_shapes=scratch,
        compiler_params=pltpu.CompilerParams(
            dimension_semantics=("arbitrary",) * len(grid), vmem_limit_bytes=VMEM_BYTES
        ),
        cost_estimate=pl.CostEstimate(flops=flops // SPEEDUP, bytes_accessed=moved // SPEEDUP, transcendentals=exps // SPEEDUP),
        name=name,
    )(*[a for a, _ in inputs])


def full(array):
    return (array, whole(array.shape))


def attention_scratch(width, keys, biased):
    heads = width // DK
    scratch = [
        pltpu.VMEM((width, keys), BF16),
        pltpu.VMEM((keys, TILE), jnp.int32),
        pltpu.VMEM((heads, keys, BQ), F32),
        pltpu.VMEM((width, BQ), F32),
    ]
    if biased:
        scratch.append(pltpu.VMEM((heads, 2 * keys - TILE, TILE), F32))
    return scratch


def transposed_spec(width):
    return pl.BlockSpec((width, BQ), lambda i: (0, i))


def self_forward(lens, x, gain, wq, wk, wv, bias, causal, name):
    seq, model = x.shape
    width = wq.shape[0]
    inputs = [(lens, SMEM_SPEC)]
    inputs += [full(a) for a in (x, gain, wq, wk, wv, bias[0], bias[1])]
    outputs = [((seq, model), BF16, whole((seq, model)))]
    outputs += [((seq, width), BF16, whole((seq, width)))] * 3
    outputs += [((seq, width), BF16, rows_spec(width)), ((8, seq), F32, lanes_spec())]
    outputs.append(((width, seq), F32, transposed_spec(width)))
    result = call(
        functools.partial(self_forward_kernel, causal), name, (seq // BQ,), inputs, outputs,
        attention_scratch(width, seq, True), 6 * seq * model * width + 2 * seq * seq * width,
        seq * seq,
    )
    return result[:6], result[6]


def order_scratch(width, model, rows):
    return [pltpu.VMEM((4, width, model), BF16), pltpu.VMEM((4, width, rows), F32)]


def piece_inputs(pieces, weights, model, half):
    width = pieces[0].shape[0]
    spec = pl.BlockSpec((width, model), lambda *_: (0, half), pipeline_mode=pl.Buffered(1))
    return [(a, transposed_spec(width)) for a in pieces] + [(a, spec) for a in weights]


def cross_forward(me, ql, kl, y0, pieces, weights, x1, enc_sum, gain, wq, wk, wv):
    seq, model = y0.shape
    width = wq.shape[0]
    inputs = [(me, SMEM_SPEC), (ql, SMEM_SPEC), (kl, SMEM_SPEC), (y0, rows_spec(model))]
    inputs += piece_inputs(pieces, weights, model, 0)
    inputs += [full(a) for a in (x1, enc_sum, gain, wq, wk, wv)]
    outputs = [
        ((seq, model), F32, rows_spec(model)),
        ((seq, model), BF16, rows_spec(model)),
        ((seq, model), BF16, whole((seq, model))),
        ((seq, width), BF16, rows_spec(width)),
        ((seq, width), BF16, whole((seq, width))),
        ((seq, width), BF16, whole((seq, width))),
        ((seq, width), BF16, rows_spec(width)),
        ((8, seq), F32, lanes_spec()),
        ((width, seq), F32, transposed_spec(width)),
    ]
    scratch = attention_scratch(width, seq, False) + order_scratch(width, model, ROWS)
    result = call(
        cross_forward_kernel, "cross_forward", (seq // BQ,), inputs, outputs, scratch,
        14 * seq * model * width + 2 * seq * seq * width, seq * seq,
    )
    return result[:8], result[8]


def row_outputs(seq, *kinds):
    return [((seq, width), dtype, rows_spec(width)) for width, dtype in kinds]


def ffn_forward(me, x, pieces, weights, gain, wi, wo):
    seq, model = x.shape
    units = wi.shape[1]
    inputs = [(me, SMEM_SPEC), (x, rows_spec(model))] + piece_inputs(pieces, weights, model, 0)
    inputs += [full(a) for a in (gain, wi, wo)]
    outputs = row_outputs(seq, (model, F32), (model, BF16), (units, F32), (units, BF16), (model, F32))
    return call(
        ffn_forward_kernel, "ffn_forward", (seq // ROWS,), inputs, outputs,
        order_scratch(weights[0].shape[0], model, ROWS), 6 * seq * model * units, seq * units,
    )


def ffn_both(me, y, pieces, weights, gain, wi, wo, cot):
    seq, model = y.shape
    units = wi.shape[1]
    inputs = [(me, SMEM_SPEC), (y, rows_spec(model))] + piece_inputs(pieces, weights, model, 1)
    inputs += [full(a) for a in (gain, wi, wo)] + [(cot, rows_spec(model))]
    outputs = row_outputs(
        seq, (model, F32), (model, BF16), (units, BF16), (units, BF16), (model, F32), (model, F32)
    )
    return call(
        ffn_both_kernel, "ffn_both", (seq // ROWS,), inputs, outputs,
        order_scratch(weights[0].shape[0], model, ROWS), 10 * seq * model * units, seq * units,
    )


def ffn_backward(cot, summed, hid, wi, wo):
    seq, units = hid.shape
    model = wi.shape[0]
    inputs = [(cot, rows_spec(model)), (summed, rows_spec(model)), (hid, rows_spec(units))]
    inputs += [full(wi), full(wo)]
    outputs = row_outputs(seq, (model, F32), (model, BF16), (units, BF16), (model, F32))
    return call(
        ffn_backward_kernel, "ffn_backward", (seq // ROWS,), inputs, outputs, [],
        4 * seq * model * units, seq * units,
    )


def closing(x0, eb, enc_gain, enc_sum, y0, sb, dec_gain, dec_sum, y2, last):
    seq, model = x0.shape
    inputs = [
        full(a) if a.shape[0] == 1 else (a, rows_spec(model))
        for a in (x0, eb, enc_gain, enc_sum, y0, sb, dec_gain, dec_sum, y2, last)
    ]
    return call(
        closing_kernel, "closing", (seq // ROWS,), inputs,
        row_outputs(seq, (model, F32), (model, F32), (model, BF16)), [], 20 * seq * model,
    )


def dot_rows(left, right):
    return lax.dot_general(
        left, right, (((0,), (0,)), ((), ())), preferred_element_type=jnp.float32
    )


def attention_weights_kernel(dq_ref, dk_ref, dv_ref, o_ref, n_ref, m_ref, g_ref, out_ref):
    count = dq_ref.shape[1]
    pairs = ((dq_ref, n_ref), (dk_ref, m_ref), (dv_ref, m_ref), (o_ref, g_ref))
    for i, (left, right) in enumerate(pairs):
        out_ref[i * count : (i + 1) * count, :] = dot_rows(left[...], right[...])


def attention_weights(grads, attended, normed, memory):
    seq, model = normed.shape
    width = attended.shape[1]
    inputs = [full(a) for a in (*grads[2:5], attended, normed, memory, grads[1])]
    outputs = [((4 * width, model), F32, whole((4 * width, model)))]
    return call(
        attention_weights_kernel, "attention_weights", (1,), inputs, outputs, [],
        8 * seq * model * width,
    )[0]


def attention_back(
    core, ql, kl, base, stream, dn, gain, wo, kept, wq, wk, wv, bias, x0, causal, name
):
    q, k, v, o, lse = kept
    seq, width = q.shape
    model = wo.shape[1]
    heads = width // DK
    biased = bias is not None
    inputs = [(core, SMEM_SPEC), (ql, SMEM_SPEC), (kl, SMEM_SPEC)]
    inputs += [(base, rows_spec(model)), (stream, rows_spec(model))]
    inputs += [(dn[0], rows_spec(model))] if len(dn) == 1 else [full(a) for a in dn]
    inputs += [full(gain), full(wo)]
    inputs += [(q, rows_spec(width)), full(k), full(v), (o, rows_spec(width)), (lse, lanes_spec())]
    inputs += [full(wq), full(wk), full(wv)]
    if biased:
        inputs += [full(bias[0]), full(bias[1]), full(x0)]
    outputs = [((seq, model), F32, rows_spec(model)), ((seq, model), BF16, rows_spec(model))]
    outputs += [((seq, width), BF16, whole((seq, width)))] * 3
    outputs.append(((1, model), F32, whole((1, model))))
    if biased:
        outputs.append((bias[1].shape, F32, whole(bias[1].shape)))
        outputs.append(((1, model), F32, whole((1, model))))
    outputs.append(((seq, model), F32, whole((seq, model))))
    if not biased:
        outputs.append(((seq, model), F32, whole((seq, model))))
    scratch = [
        pltpu.VMEM((width, seq), BF16),
        pltpu.VMEM((seq, TILE), jnp.int32),
        pltpu.VMEM((width, BQ), F32),
        pltpu.VMEM((seq, width), F32),
        pltpu.VMEM((seq, width), F32),
    ]
    if biased:
        scratch += [pltpu.VMEM((heads, 2 * seq - TILE, TILE), F32)] * 2
    result = call(
        functools.partial(attention_back_kernel, causal, biased, len(dn)),
        name, (seq // BQ,), inputs,
        outputs, scratch, 8 * seq * model * width + 5 * seq * seq * width, seq * seq,
    )
    return result[:6], result[6:]


MESH_ID = pl.DeviceIdType.MESH
MB_PER_ROW = 0.768 * 4 / 1000
RATES = (2.0, 21.0, 21.3, 21.5, 44.0)
DEPTH = 2


class Copies:
    def __init__(self, send_sem, recv_sem):
        self.send_sem, self.recv_sem = send_sem, recv_sem
        self.all, self.steps, self.first = [], [], []

    def copy(self, source, target, axis, index, link, rows, stage=0):
        i = len(self.all)

        def make():
            return pltpu.make_async_remote_copy(
                src_ref=source,
                dst_ref=target,
                send_sem=self.send_sem.at[i],
                recv_sem=self.recv_sem.at[i],
                device_id={axis: index},
                device_id_type=MESH_ID,
            )

        self.all.append((make, link, rows, stage))
        return i

    def step(self, waits, work, starts):
        self.steps.append((waits, work, starts))

    def start(self, i):
        make, link, rows, _ = self.all[i]
        self.made[i] = make()
        self.made[i].start()
        begin = max(self.now, self.free.get(link, 0.0))
        if link == 4:
            half = 22.0 * rows * MB_PER_ROW
            begin = max(begin, self.free.get(3, 0.0) - half)
            self.free[3] = max(self.free.get(3, 0.0), begin) + half
        self.free[link] = begin + RATES[link] * rows * MB_PER_ROW
        self.arrive[i] = self.free[link] + 1.0

    def fill(self):
        for i in sorted(self.pending, key=lambda i: (-self.all[i][3], i)):
            link = self.all[i][1]
            busy = sum(self.all[j][1] == link and self.arrive[j] > self.now for j in self.made)
            if busy < DEPTH or link < 2:
                self.pending.remove(i)
                self.start(i)

    def run(self):
        self.now, self.free, self.arrive, self.made = 0.0, {}, {}, {}
        self.pending = list(self.first)
        left = list(self.steps)
        self.fill()
        while left:
            ready = [s for s in left if all(i in self.made for i in s[0])]
            step = min(ready, key=lambda s: max([self.arrive[i] for i in s[0]], default=0.0))
            left.remove(step)
            for i in step[0]:
                self.made[i].wait_recv()
                self.now = max(self.now, self.arrive[i])
            if step[1] is not None:
                step[1]()
            self.pending += step[2]
            self.fill()
        for made in self.made.values():
            made.wait_send()


def mp_partners():
    me = lax.axis_index("mp")
    core = lax.rem(me, 2)
    return core, me + 1 - 2 * core, lax.rem(me + 2, 4)


def dp_side(bit):
    return lax.rem(lax.axis_index("dp") // (1 << bit), 2)


def dp_partner(bit):
    return lax.axis_index("dp") + (1 << bit) * (1 - 2 * dp_side(bit))


def greet(bits):
    barrier = pltpu.get_barrier_semaphore()
    _, beside, across = mp_partners()
    ids = [{"mp": beside}, {"mp": across}] + [{"dp": dp_partner(bit)} for bit in bits]
    for device_id in ids:
        pl.semaphore_signal(barrier, inc=1, device_id=device_id, device_id_type=MESH_ID)
    pl.semaphore_wait(barrier, len(ids))


def rows_at(start, count):
    return pl.ds(pl.multiple_of(start, 8), count)


def mp_job(copies, part_ref, near_ref, far_ref, out_ref, chunks, finish=None, far=True):
    core, beside, across = mp_partners()
    count = part_ref.shape[0] // (2 * chunks)

    def one(k):
        mine = rows_at((2 * k + core) * count, count)
        other = rows_at((2 * k + 1 - core) * count, count)
        first = copies.copy(part_ref.at[other, :], near_ref.at[k], "mp", beside, 0, count)
        copies.first.append(first)

        def add_near():
            near_ref[k] = part_ref[mine, :] + near_ref[k]

        second = copies.copy(near_ref.at[k], far_ref.at[k], "mp", across, 1, count)
        copies.step([first], add_near, [second])

        def add_far():
            out_ref[mine, :] = near_ref[k] + far_ref[k]
            if finish is not None:
                finish(mine)

        third = copies.copy(out_ref.at[mine, :], out_ref.at[mine, :], "mp", beside, 0, count)
        copies.step([second], add_far, [third])
        copies.step([third], None if finish is None else lambda: finish(other), [])

    for k in range(chunks):
        one(k)


def near_job(copies, part_ref, land_ref, out_ref):
    core, beside, _ = mp_partners()
    count = part_ref.shape[0] // 2
    mine = rows_at(core * count, count)
    other = rows_at((1 - core) * count, count)
    first = copies.copy(part_ref.at[other, :], land_ref, "mp", beside, 0, count)
    copies.first.append(first)

    def add():
        out_ref[...] = part_ref[mine, :] + land_ref[...]

    copies.step([first], add, [])


LINKS = (2, 3, 4)


def scatter_job(copies, part_ref, land_refs, bits, base, rows, store, got_ref=None):
    start, count, waits, work = base, rows, None, None
    source, origin = part_ref, 0
    for level, bit in enumerate(bits):
        count = count // 2
        side = dp_side(bit)
        keep = start + side * count
        give = start + (1 - side) * count
        land = land_refs[level]
        place = base // rows * count
        landing = slice(place, place + count)
        got = land
        if level == 0 and got_ref is not None:
            made, got = None, got_ref
        else:
            made = copies.copy(
                source.at[rows_at(give - origin, count), :], land.at[landing, :], "dp",
                dp_partner(bit), LINKS[min(bit, 2)], count, level,
            )
            if level == 0:
                copies.first.append(made)
            else:
                copies.step(waits, work, [made])

        def work(
            source=source, origin=origin, keep=keep, land=land, got=got, landing=landing, count=count
        ):
            land[landing, :] = source[rows_at(keep - origin, count), :] + got[landing, :]

        waits = [] if made is None else [made]
        source, origin, start = land, keep - place, keep

    def last(add=work, land=land, landing=landing, start=start, count=count):
        add()
        store(start, count, land[landing, :])

    return waits, last


def gather_job(copies, out_ref, bits, base, rows, waits, work):
    count = rows >> len(bits)
    start, size = base, rows
    for bit in bits:
        size = size // 2
        start = start + dp_side(bit) * size
    for level, bit in enumerate(reversed(bits)):
        held = rows_at(start, count)
        made = copies.copy(
            out_ref.at[held, :], out_ref.at[held, :], "dp", dp_partner(bit),
            LINKS[min(bit, 2)], count, len(bits) + level,
        )
        if waits is None:
            work()
            copies.first.append(made)
        else:
            copies.step(waits, work, [made])
        waits, work = [made], None
        start = start - dp_side(bit) * count
        count = count * 2
    copies.step(waits, None, [])


def small_job(copies, small_ref, land_ref, held_ref, out_ref, bits, shared):
    core, beside, across = mp_partners()
    hops = [("mp", beside, 0), ("mp", across, 1)]
    hops += [("dp", dp_partner(bit), LINKS[min(bit, 2)]) for bit in bits]
    count = small_ref.shape[0]
    first_rows = lax.broadcasted_iota(jnp.int32, small_ref.shape, 0) < shared
    source, waits, work = small_ref, None, None
    for i, (axis, index, link) in enumerate(hops):
        made = copies.copy(source, land_ref.at[i], axis, index, link, count)
        if i == 0:
            copies.first.append(made)
        else:
            copies.step(waits, work, [made])

        def work(i=i, source=source, last=i == len(hops) - 1):
            got = land_ref[i]
            if i < 2:
                got = jnp.where(first_rows, got, 0.0)
            target = out_ref if last else held_ref.at[i]
            target[...] = source[...] + got

        waits, source = [made], held_ref.at[i]
    copies.step(waits, work, [])


CHUNKS = 4
PIECES = 4


def sums(number, parts=(), near=(), scatter=(), gather=(), units=(), turns=(), halves=(), small=None, shared=0):
    bits = list(range((lax.axis_size("dp") - 1).bit_length()))
    turned = bits[1:] + bits[:1]
    dp = bool(scatter or gather or units or small is not None)
    smalls = [] if small is None else [small]
    inputs = [*parts, *near, *scatter, *gather, *units, *smalls, *halves]
    model = inputs[0].shape[1]
    shares = lax.axis_size("dp")
    outputs = [(a.shape, F32) for a in parts]
    outputs += [((a.shape[0] // 2, model), F32) for a in near]
    outputs += [((a.shape[0] // shares, model), F32) for a in scatter]
    outputs += [((a.shape[0] * shares, model), F32) for a in gather]
    outputs += [(a.shape, F32) for a in (*units, *smalls)]
    lands = []
    for a in parts:
        lands += [pltpu.VMEM((CHUNKS, a.shape[0] // (2 * CHUNKS), model), F32)] * 2
    for a in near:
        lands.append(pltpu.VMEM((a.shape[0] // 2, model), F32))
    for a in (*scatter, *units):
        lands += [pltpu.VMEM((a.shape[0] >> (i + 1), model), F32) for i in range(len(bits))]
    for a in smalls:
        lands += [pltpu.VMEM((2 + len(bits), *a.shape), F32)] * 2
    count, ends = len(inputs), len(inputs) + len(outputs)
    total = 3 * CHUNKS * len(parts) + len(near) + len(smalls) * (2 + len(bits))
    total += len(bits) * PIECES * (len(scatter) + len(gather) + 2 * len(units))

    def kernel(*refs):
        ins, outs = list(refs[:count]), list(refs[count:ends])
        scratch = list(refs[ends:-2])
        half_refs = [None] * (len(units) - len(halves)) + ins[count - len(halves) :]
        greet(bits if dp else [])
        copies = Copies(refs[-2], refs[-1])
        for _ in parts:
            mp_job(copies, ins.pop(0), scratch.pop(0), scratch.pop(0), outs.pop(0), CHUNKS)
        for _ in near:
            near_job(copies, ins.pop(0), scratch.pop(0), outs.pop(0))
        for a in scatter:
            part_ref, out_ref = ins.pop(0), outs.pop(0)
            land_refs = [scratch.pop(0) for _ in bits]
            rows = a.shape[0] // PIECES
            for piece in range(PIECES):

                def keep(start, count, value, piece=piece, out_ref=out_ref):
                    out_ref[piece * count : (piece + 1) * count, :] = value

                waits, work = scatter_job(
                    copies, part_ref, land_refs, bits, piece * rows, rows, keep
                )
                copies.step(waits, work, [])
        for a in gather:
            part_ref, out_ref = ins.pop(0), outs.pop(0)
            rows = a.shape[0] * shares // PIECES
            for piece in range(PIECES):
                start, size = piece * rows, rows
                for bit in bits:
                    size = size // 2
                    start = start + dp_side(bit) * size

                def put(start=start, size=size, piece=piece, part_ref=part_ref, out_ref=out_ref):
                    out_ref[rows_at(start, size), :] = part_ref[
                        piece * size : (piece + 1) * size, :
                    ]

                gather_job(copies, out_ref, bits, piece * rows, rows, None, put)
        for a, half_ref in zip(units, half_refs):
            part_ref, out_ref = ins.pop(0), outs.pop(0)
            land_refs = [scratch.pop(0) for _ in bits]
            rows = a.shape[0] // PIECES
            for piece in range(PIECES):

                def keep(start, count, value, out_ref=out_ref):
                    out_ref[rows_at(start, count), :] = value

                order = turned if piece in turns else bits
                waits, work = scatter_job(
                    copies, part_ref, land_refs, order, piece * rows, rows, keep, half_ref
                )
                gather_job(copies, out_ref, order, piece * rows, rows, waits, work)
        if small is not None:
            small_job(copies, ins[0], scratch[0], scratch[1], outs[0], bits, shared)
        copies.run()

    result = pl.pallas_call(
        kernel,
        in_specs=[whole(a.shape) for a in inputs],
        out_specs=[whole(shape) for shape, _ in outputs],
        out_shape=[jax.ShapeDtypeStruct(shape, dtype) for shape, dtype in outputs],
        grid=(1,),
        scratch_shapes=lands
        + [pltpu.SemaphoreType.DMA((total,)), pltpu.SemaphoreType.DMA((total,))],
        compiler_params=pltpu.CompilerParams(
            collective_id=number, has_side_effects=True, vmem_limit_bytes=VMEM_BYTES
        ),
        cost_estimate=pl.CostEstimate(flops=1, bytes_accessed=1, transcendentals=0),
        name="sums",
    )(*inputs)
    groups = []
    for group in (parts, near, scatter, gather, units, smalls):
        groups.append(list(result[: len(group)]))
        result = result[len(group) :]
    return groups


def first_half(unit):
    rows = unit.shape[0] // (2 * PIECES)
    pieces = unit.reshape(PIECES, 2, rows, unit.shape[1])
    other = 1 - lax.rem(lax.axis_index("dp"), 2)
    return lax.dynamic_index_in_dim(pieces, other, 1, False).reshape(PIECES * rows, -1)


def first_swap(value):
    pairs = [(i, i ^ 1) for i in range(lax.axis_size("dp"))]
    return lax.ppermute(value, "dp", pairs)


def shares_fit(rows):
    return rows % (8 * PIECES * lax.axis_size("dp")) == 0


CORE_SWAP = [(0, 1), (1, 0), (2, 3), (3, 2)]
CHIP_SWAP = [(0, 2), (2, 0), (1, 3), (3, 1)]


def core_swap(value):
    return lax.ppermute(value, "mp", CORE_SWAP)


def chip_swap(value):
    return lax.ppermute(value, "mp", CHIP_SWAP)


def part(value, start, rows):
    return lax.dynamic_slice_in_dim(value, start, rows, axis=0)


class Chain:
    def __init__(self):
        self.token = None

    def tie(self, value):
        if self.token is None:
            return value
        value, _ = lax.optimization_barrier((value, self.token))
        return value

    def mark(self, value):
        self.token = value


class Wire:
    def __init__(self, chain, swap):
        self.chain, self.swap = chain, swap

    def send(self, value):
        self.value = self.swap(self.chain.tie(value))

    def wait(self):
        self.value = self.chain.tie(self.value)
        self.chain.mark(self.value)
        return self.value


class Gather:
    def __init__(self, chain):
        self.chain = chain
        self.y, self.s, self.r = [Wire(chain, swap) for swap in (chip_swap, core_swap, core_swap)]

    def put(self, own):
        self.own = own

    def sy(self):
        self.y.send(self.own)

    def wy(self):
        self.y.wait()

    def ss(self):
        self.s.send(self.own)

    def ws(self):
        self.s.wait()

    def sr(self):
        self.r.send(self.y.value)

    def wr(self):
        self.r.wait()

    def pieces(self):
        return (self.own, self.y.value, self.s.value, self.r.value)


def project_weight(left, right):
    return lax.dot_general(
        left, right, (((0,), (0,)), ((), ())), preferred_element_type=jnp.float32
    )


def signed_buckets(buckets, seq):
    fill = jnp.full((2 * seq - buckets.shape[0],), -1, jnp.int32)
    return jnp.concatenate([fill, buckets])[None, :]


def body(
    encoder_input,
    decoder_input,
    encoder_lengths,
    decoder_lengths,
    encoder_buckets,
    decoder_buckets,
    encoder_attn_gain,
    encoder_query,
    encoder_key,
    encoder_value,
    encoder_output,
    encoder_bias,
    encoder_ffn_gain,
    encoder_ffn_in,
    encoder_ffn_out,
    decoder_attn_gain,
    decoder_query,
    decoder_key,
    decoder_value,
    decoder_output,
    decoder_bias,
    cross_gain,
    cross_query,
    cross_key,
    cross_value,
    cross_output,
    decoder_ffn_gain,
    decoder_ffn_in,
    decoder_ffn_out,
    encoder_cotangent,
    decoder_cotangent,
):
    _, seq, width = encoder_input.shape
    enc_lens, dec_lens = encoder_lengths, decoder_lengths
    enc_bias = (signed_buckets(encoder_buckets, seq), encoder_bias)
    dec_bias = (signed_buckets(decoder_buckets, seq), decoder_bias)
    me = lax.axis_index("mp").astype(jnp.int32).reshape(1)
    core = lax.rem(me, 2)
    x0, y0 = encoder_input[0], decoder_input[0]
    enc_cot, dec_cot = encoder_cotangent[0], decoder_cotangent[0]
    row = lambda gain: gain[None, :]
    encoder_query, encoder_key, encoder_value = encoder_query.T, encoder_key.T, encoder_value.T
    decoder_query, decoder_key, decoder_value = decoder_query.T, decoder_key.T, decoder_value.T
    cross_query, cross_key, cross_value = cross_query.T, cross_key.T, cross_value.T
    chain = Chain()
    tie, mark = chain.tie, chain.mark

    wide_e, wide, e, d, x = [Gather(chain) for _ in range(5)]
    wide_e.put(encoder_output.astype(F32))
    mark(wide_e.own)
    wide_e.sy()
    count = encoder_output.shape[0] // lax.axis_size("dp")
    place = lax.axis_index("dp") * count
    slices = Wire(chain, chip_swap)
    slices.send(
        jnp.concatenate(
            [part(decoder_output, place, count), part(cross_output, place, count)], axis=1
        ).astype(F32)
    )
    enc, out = self_forward(
        enc_lens, tie(x0), row(encoder_attn_gain), encoder_query, encoder_key, encoder_value,
        enc_bias, False, "encoder_attention",
    )
    mark(out)
    e.put(out)
    wide_e.wy()
    slices.wait()
    e.sy()
    e.ss()
    wide.y.value = lax.all_gather(tie(slices.value), "dp", axis=0, tiled=True)
    wide_e.sr()
    wide_e.ss()

    dec, out = self_forward(
        dec_lens, tie(y0), row(decoder_attn_gain), decoder_query, decoder_key, decoder_value,
        dec_bias, True, "decoder_attention",
    )
    mark(out)
    d.put(out)
    e.wy()
    e.sr()
    d.sy()
    e.ws()
    wide_e.ws()
    wide_e.wr()
    e.wr()
    own = jnp.concatenate([decoder_output, cross_output], axis=1).astype(F32)
    wide.put(own)

    ffn = ffn_forward(
        me, tie(x0), e.pieces(), wide_e.pieces(), row(encoder_ffn_gain), encoder_ffn_in,
        encoder_ffn_out,
    )
    mark(ffn[4])
    d.wy()
    d.ss()
    d.sr()
    wide.ss()
    enc_sum = sums(1, parts=[tie(ffn[4])])[0][0]
    mark(enc_sum)
    wide.sr()
    d.ws()
    d.wr()
    wide.ws()
    wide.wr()

    cross, out = cross_forward(
        me, dec_lens, enc_lens, tie(y0), d.pieces(), wide.pieces(), ffn[0], enc_sum, row(cross_gain),
        cross_query, cross_key, cross_value,
    )
    mark(out)
    x.put(out)
    x.sy()
    x.ss()
    x.wy()
    x.sr()
    x.ws()
    x.wr()

    both = ffn_both(
        me, tie(cross[0]), x.pieces(), wide.pieces(), row(decoder_ffn_gain), decoder_ffn_in,
        decoder_ffn_out, dec_cot,
    )
    mark(both[4])
    dn = sums(2, parts=[tie(both[4])])[0][0]
    mark(dn)

    cb, (own_part, memory_part) = attention_back(
        core, dec_lens, enc_lens, dec_cot, both[0], (tie(dn),), row(decoder_ffn_gain),
        cross_output, cross[3:8], cross_query, cross_key, cross_value, None, None, False,
        "cross_back",
    )
    mark(own_part)
    unit_1a = project_weight(tie(both[1]), both[3])
    unit_1b = project_weight(both[2], dec_cot)
    unit_2 = attention_weights((*cb[:2], tie(cb[2]), *cb[3:]), cross[6], cross[1], cross[2])
    mark(unit_2)
    unit_1a = tie(unit_1a)
    mark(unit_1a)
    unit_1a, unit_1b, unit_2 = lax.psum((unit_1a, unit_1b, unit_2), "dp")
    split_units = shares_fit(width)
    totals, nears, _, _, _, _ = sums(3, parts=[tie(memory_part)], near=[own_part])
    grad_memory, own_near = totals[0], nears[0]
    mark(grad_memory)

    back = ffn_backward(enc_cot, tie(grad_memory), ffn[2], encoder_ffn_in, encoder_ffn_out)
    mark(back[3])
    unit_4a = project_weight(tie(ffn[1]), back[2])
    mark(unit_4a)
    unit_4b = project_weight(tie(ffn[3]), back[1])
    mark(unit_4b)
    totals, _, shares, _, _, _ = sums(
        4, parts=[tie(back[3])], scatter=[unit_4a] if split_units else []
    )
    dn = totals[0]
    mark(dn)
    half_4b, half_5 = [Wire(chain, first_swap) for _ in range(2)]
    half_4b.send(first_half(unit_4b))
    own_far, own_beside, own_relay = [
        Wire(chain, swap) for swap in (chip_swap, core_swap, core_swap)
    ]
    own_far.send(own_near)
    own_beside.send(own_near)

    eb, (enc_table, enc_gain, enc_part) = attention_back(
        core, enc_lens, enc_lens, back[0], ffn[0], (tie(dn),), row(encoder_ffn_gain),
        encoder_output, enc[1:6], encoder_query, encoder_key, encoder_value, enc_bias, x0, False,
        "encoder_back",
    )
    mark(enc_part)
    own_beside.wait()
    own_far.wait()
    own_relay.send(own_far.value)
    half_4b.wait()
    unit_5 = attention_weights((*eb[:2], tie(eb[2]), *eb[3:]), enc[4], enc[0], enc[0])
    mark(unit_5)
    half_5.send(first_half(unit_5))
    own_relay.wait()

    own_pieces = (own_near, own_far.value, own_beside.value, own_relay.value)
    sb, (dec_table, dec_gain, dec_part) = attention_back(
        core, dec_lens, dec_lens, tie(cb[0]), cross[0], own_pieces, row(cross_gain),
        decoder_output, dec[1:6], decoder_query, decoder_key, decoder_value, dec_bias, y0, True,
        "decoder_back",
    )
    mark(dec_part)
    half_5.wait()
    unit_3 = attention_weights((*sb[:2], tie(sb[2]), *sb[3:]), dec[4], dec[0], dec[0])
    tables = []
    for table in (enc_table, dec_table):
        flat = table.reshape(1, -1)
        tables.append(jnp.pad(flat, ((0, 0), (0, width - flat.shape[1]))))
    blank = jnp.zeros((1, width), F32)
    small = jnp.concatenate([enc_gain, dec_gain, eb[5], sb[5], cb[5], *tables, blank], axis=0)
    units = [unit_3, unit_4b, unit_5] if split_units else []
    halves = [half_4b.value, half_5.value] if split_units else []
    totals, _, _, gathered, units, smalls = sums(
        5, parts=[enc_part, dec_part, both[5]], gather=shares, units=units, halves=halves,
        small=small, shared=2
    )
    small = smalls[0]
    if split_units:
        unit_4a = gathered[0]
        unit_3, unit_4b, unit_5 = units
    else:
        unit_4a, unit_3, unit_4b, unit_5 = lax.psum((unit_4a, unit_3, unit_4b, unit_5), "dp")
    enc_grad, dec_grad, result = closing(
        x0, eb[0], row(encoder_attn_gain), totals[0], y0, sb[0], row(decoder_attn_gain), totals[1],
        both[0], totals[2],
    )

    def matrices(stack):
        count = stack.shape[0] // 4
        pieces = [stack[i * count : (i + 1) * count] for i in range(4)]
        return [jnp.transpose(piece) for piece in pieces[:3]] + pieces[3:]

    shape = encoder_bias.shape
    count = shape[0] * shape[1]
    return (
        cross[2][None],
        result[None],
        enc_grad[None],
        dec_grad[None],
        small[0],
        *matrices(unit_5),
        small[5, :count].reshape(shape),
        small[2],
        unit_4a,
        unit_4b,
        small[1],
        *matrices(unit_3),
        small[6, :count].reshape(shape),
        small[3],
        *matrices(unit_2),
        small[4],
        unit_1a,
        unit_1b,
    )


def solution(mesh):
    return jax.shard_map(
        body,
        mesh=mesh,
        in_specs=(
            P("dp", None, None),
            P("dp", None, None),
            P("dp", None),
            P("dp", None),
            P(),
            P(),
            P(),
            P(None, "mp"),
            P(None, "mp"),
            P(None, "mp"),
            P("mp", None),
            P(None, "mp"),
            P(),
            P(None, "mp"),
            P("mp", None),
            P(),
            P(None, "mp"),
            P(None, "mp"),
            P(None, "mp"),
            P("mp", None),
            P(None, "mp"),
            P(),
            P(None, "mp"),
            P(None, "mp"),
            P(None, "mp"),
            P("mp", None),
            P(),
            P(None, "mp"),
            P("mp", None),
            P("dp", None, None),
            P("dp", None, None),
        ),
        out_specs=(
            P("dp", None, None),
            P("dp", None, None),
            P("dp", None, None),
            P("dp", None, None),
            P(),
            P(None, "mp"),
            P(None, "mp"),
            P(None, "mp"),
            P("mp", None),
            P(None, "mp"),
            P(),
            P(None, "mp"),
            P("mp", None),
            P(),
            P(None, "mp"),
            P(None, "mp"),
            P(None, "mp"),
            P("mp", None),
            P(None, "mp"),
            P(),
            P(None, "mp"),
            P(None, "mp"),
            P(None, "mp"),
            P("mp", None),
            P(),
            P(None, "mp"),
            P("mp", None),
        ),
        check_vma=False,
    )
```

```python
import functools

import jax
import jax.numpy as jnp
from jax import lax
from jax.experimental import pallas as pl
from jax.experimental.pallas import tpu as pltpu
from jax.sharding import PartitionSpec as P

DK = 64
EPS = 1e-06
NEG = -1e30
HIGHEST = lax.Precision.HIGHEST
TILE = 128
BQ = 256
KC = 256
SPEEDUP = 1 << 20
VMEM_BYTES = 60 * 1024 * 1024


def doc_ends(lens_ref):
    ends = []
    total = jnp.int32(0)
    for j in range(lens_ref.shape[1]):
        total = total + lens_ref[0, j]
        ends.append(total)
    return ends


def docs_at(places, ends):
    result = jnp.zeros(places.shape, jnp.int32)
    for end in ends:
        result = result + (places >= end).astype(jnp.int32)
    return result


def key_range(ql_ref, q_ends, kl_ref, block, causal):
    first = block * BQ
    last = first + BQ - 1
    low = jnp.int32(0)
    high = jnp.int32(0)
    for j, end in enumerate(q_ends):
        low = low + jnp.where(end <= first, kl_ref[0, j], 0)
        high = high + jnp.where(end - ql_ref[0, j] <= last, kl_ref[0, j], 0)
    if causal:
        high = jnp.minimum(high, first + BQ)
    return low // KC, (high + KC - 1) // KC


def bucket_hits(buckets_ref, count):
    ids = lax.broadcasted_iota(jnp.int32, (count, buckets_ref.shape[1]), 0)
    return ids == buckets_ref[...]


def make_tiles(buckets_ref, table_ref, tiles_ref):
    hits = bucket_hits(buckets_ref, table_ref.shape[0])
    width = buckets_ref.shape[1]
    for h in range(tiles_ref.shape[0]):
        row = jnp.sum(jnp.where(hits, table_ref[:, h : h + 1], 0.0), axis=0, keepdims=True)
        row = jnp.where(buckets_ref[...] < 0, NEG, row)
        for k in range(tiles_ref.shape[1] // TILE):
            start = width - 2 * TILE - k * TILE
            window = jnp.broadcast_to(row[:, start : start + 2 * TILE], (TILE, 2 * TILE))
            skewed = pltpu.roll(window, 0, 1, stride=1, stride_axis=0)
            tiles_ref[h, k * TILE : (k + 1) * TILE, :] = skewed[:, TILE:]


def sum_tiles(buckets_ref, grad_tiles_ref, grad_table_ref):
    count = grad_table_ref.shape[0]
    width = buckets_ref.shape[1]
    hits = bucket_hits(buckets_ref, count)
    blocks = grad_tiles_ref.shape[1] // TILE
    blank = jnp.zeros((8, TILE), jnp.float32)
    for h in range(grad_tiles_ref.shape[0]):
        halves = []
        for k in range(blocks):
            total = jnp.zeros((8, 2 * TILE), jnp.float32)
            for a in range(0, TILE, 8):
                piece = grad_tiles_ref[h, k * TILE + a : k * TILE + a + 8, :]
                wide = jnp.concatenate([blank, piece], axis=1)
                total = total + pltpu.roll(wide, (2 * TILE - a) % (2 * TILE), 1)
            halves.append(total)
        parts = []
        for m in range(width // TILE):
            upper = halves[blocks - 1 - m][:, :TILE] if m < blocks else None
            lower = halves[blocks - m][:, TILE:] if m >= 1 else None
            part = upper if lower is None else lower if upper is None else upper + lower
            parts.append(part)
        group = jnp.concatenate(parts, axis=1)
        row = group[0:1]
        for b in range(1, 8):
            row = row + pltpu.roll(group[b : b + 1], width - b, 1)
        grad_table_ref[:, h : h + 1] = jnp.sum(jnp.where(hits, row, 0.0), axis=1, keepdims=True)


def tile_rows(tiles_ref, h, block, chunk, keys):
    parts = []
    for t in range(BQ // TILE):
        start = keys - TILE - TILE * (block * (BQ // TILE) + t) + chunk * KC
        parts.append(tiles_ref[h, pl.ds(pl.multiple_of(start, TILE), KC), :])
    return jnp.concatenate(parts, axis=1)


def head_mask(h, width):
    lane = lax.broadcasted_iota(jnp.int32, (1, width), 1)
    return ((lane >= h * DK) & (lane < (h + 1) * DK)).astype(jnp.bfloat16)


def dot_last(left, right):
    return lax.dot_general(
        left, right, (((1,), (1,)), ((), ())), preferred_element_type=jnp.float32
    )


def dot(left, right):
    return jnp.dot(left, right, preferred_element_type=jnp.float32)


def flip(value):
    return jnp.transpose(value.astype(jnp.float32)).astype(value.dtype)


ROWS = 256


def ref_norm(stream, gain):
    scale = lax.rsqrt(jnp.mean(stream * stream, axis=-1, keepdims=True) + EPS)
    return stream * scale * gain


def norm_back(stream, gain, grad_normed):
    scale = lax.rsqrt(jnp.mean(stream * stream, axis=-1, keepdims=True) + EPS)
    unit = stream * scale
    scaled = gain * grad_normed
    grad = scale * (scaled - unit * jnp.mean(scaled * unit, axis=-1, keepdims=True))
    return grad, jnp.sum(grad_normed * unit, axis=0, keepdims=True)


GELU_SCALE = 0.7978845608028654
GELU_CUBE = 0.044715


def gelu_parts(value):
    square = value * value
    curve = jnp.tanh(GELU_SCALE * (value + GELU_CUBE * value * square))
    active = 0.5 * value * (1.0 + curve)
    slope = 0.5 * (1.0 + curve) + 0.5 * value * (1.0 - curve * curve) * GELU_SCALE * (
        1.0 + 3.0 * GELU_CUBE * square
    )
    return active, slope


def block_rows(index):
    return pl.ds(pl.multiple_of(index * ROWS, ROWS), ROWS)


def attend_block(block, causal, biased, ql_ref, kl_ref, q_block, k_ref, vt_ref, kd_ref, s_ref, o_acc, tiles_ref, lse_ref):
    keys, width = k_ref.shape
    heads = width // DK
    q_ends = doc_ends(ql_ref)
    q_docs = docs_at(block * BQ + lax.broadcasted_iota(jnp.int32, (1, BQ), 1), q_ends)
    queries = q_block * jnp.bfloat16(DK ** (-0.5))
    masked = [queries * head_mask(h, width) for h in range(heads)]
    low, high = key_range(ql_ref, q_ends, kl_ref, block, causal)

    def first(chunk, tops):
        rows = pl.ds(pl.multiple_of(chunk * KC, KC), KC)
        docs = jnp.concatenate([kd_ref[rows, :]] * (BQ // TILE), axis=1)
        allowed = docs == q_docs
        fresh = []
        for h in range(heads):
            scores = dot_last(k_ref[rows, :], masked[h])
            if biased:
                scores = scores + tile_rows(tiles_ref, h, block, chunk, keys)
            scores = jnp.where(allowed, scores, NEG)
            s_ref[h, rows, :] = scores
            fresh.append(jnp.maximum(tops[h], jnp.max(scores, axis=0, keepdims=True)))
        return tuple(fresh)

    tops = lax.fori_loop(
        low, high, first, tuple(jnp.full((1, BQ), NEG, jnp.float32) for _ in range(heads))
    )
    o_acc[...] = jnp.zeros_like(o_acc)

    def second(chunk, totals):
        rows = pl.ds(pl.multiple_of(chunk * KC, KC), KC)
        fresh = []
        for h in range(heads):
            probs = jnp.exp(s_ref[h, rows, :] - tops[h])
            fresh.append(totals[h] + jnp.sum(probs, axis=0, keepdims=True))
            o_acc[h * DK : (h + 1) * DK, :] += dot(
                vt_ref[h * DK : (h + 1) * DK, rows], probs.astype(jnp.bfloat16)
            )
        return tuple(fresh)

    totals = lax.fori_loop(
        low, high, second, tuple(jnp.zeros((1, BQ), jnp.float32) for _ in range(heads))
    )
    outs = []
    for h in range(heads):
        lse_ref[h : h + 1, :] = tops[h] + jnp.log(totals[h])
        outs.append(o_acc[h * DK : (h + 1) * DK, :] / totals[h])
    return jnp.concatenate(outs, axis=0).astype(jnp.bfloat16).astype(jnp.float32)


def put_out(out, o_ref, ot_ref):
    o_ref[...] = jnp.transpose(out).astype(jnp.bfloat16)
    ot_ref[...] = out


def order_pieces(me, own, far, sib, sibfar, target_ref):
    other = lax.rem(me + 2, 4)
    beside = me + 1 - 2 * lax.rem(me, 2)
    target_ref[me] = own
    target_ref[other] = far
    target_ref[beside] = sib
    target_ref[lax.rem(beside + 2, 4)] = sibfar


def order_weights(me, refs, target_ref):
    order_pieces(me, *[ref[...].astype(jnp.bfloat16) for ref in refs], target_ref)


def out_product(me, refs, lanes, weights_ref, pieces_ref):
    order_pieces(me, *[ref[:, lanes] for ref in refs], pieces_ref)
    total = None
    for m in range(4):
        left = jnp.transpose(pieces_ref[m]).astype(jnp.bfloat16)
        product = dot(left, weights_ref[m])
        total = product if total is None else total + product
    return total


def self_forward_kernel(causal, *refs):
    ql_ref, x_ref, gain_ref, wq_ref, wk_ref, wv_ref, buckets_ref, table_ref = refs[:8]
    n_ref, q_ref, k_ref, v_ref, o_ref, lse_ref = refs[8:14]
    ot_ref = refs[14]
    vt_ref, kd_ref, s_ref, o_acc, tiles_ref = refs[15:]
    block = pl.program_id(0)
    keys = k_ref.shape[0]

    @pl.when(block == 0)
    def _():
        for b in range(keys // ROWS):
            rows = slice(b * ROWS, (b + 1) * ROWS)
            normed = ref_norm(x_ref[rows, :].astype(jnp.float32), gain_ref[...]).astype(
                jnp.bfloat16
            )
            n_ref[rows, :] = normed
            q_ref[rows, :] = dot_last(normed, wq_ref[...]).astype(jnp.bfloat16)
            k_ref[rows, :] = dot_last(normed, wk_ref[...]).astype(jnp.bfloat16)
            value = dot_last(normed, wv_ref[...])
            v_ref[rows, :] = value.astype(jnp.bfloat16)
            vt_ref[:, rows] = jnp.transpose(value).astype(jnp.bfloat16)
        kd_ref[...] = docs_at(
            lax.broadcasted_iota(jnp.int32, (keys, TILE), 0), doc_ends(ql_ref)
        )
        make_tiles(buckets_ref, table_ref, tiles_ref)

    out = attend_block(
        block, causal, True, ql_ref, ql_ref, q_ref[block_rows(block), :],
        k_ref, vt_ref, kd_ref, s_ref, o_acc, tiles_ref, lse_ref,
    )
    put_out(out, o_ref, ot_ref)


def cross_forward_kernel(*refs):
    me_ref, ql_ref, kl_ref, y0_ref = refs[:4]
    dec_pieces, dec_weights = refs[4:8], refs[8:12]
    x1_ref, enc_sum_ref, gain_ref, wq_ref, wk_ref, wv_ref = refs[12:18]
    y1_ref, n_ref, memory_ref, q_ref, k_ref, v_ref, o_ref, lse_ref, ot_ref = refs[18:27]
    vt_ref, kd_ref, s_ref, o_acc, weights_ref, pieces_ref = refs[27:]
    block = pl.program_id(0)
    keys = k_ref.shape[0]
    me = me_ref[0]

    @pl.when(block == 0)
    def _():
        for b in range(keys // ROWS):
            rows = slice(b * ROWS, (b + 1) * ROWS)
            memory = (x1_ref[rows, :] + enc_sum_ref[rows, :]).astype(jnp.bfloat16)
            memory_ref[rows, :] = memory
            k_ref[rows, :] = dot_last(memory, wk_ref[...]).astype(jnp.bfloat16)
            value = dot_last(memory, wv_ref[...])
            v_ref[rows, :] = value.astype(jnp.bfloat16)
            vt_ref[:, rows] = jnp.transpose(value).astype(jnp.bfloat16)
        kd_ref[...] = docs_at(
            lax.broadcasted_iota(jnp.int32, (keys, TILE), 0), doc_ends(kl_ref)
        )
        order_weights(me, dec_weights, weights_ref)

    summed = out_product(me, dec_pieces, slice(None), weights_ref, pieces_ref)
    stream = y0_ref[...].astype(jnp.float32) + summed
    y1_ref[...] = stream
    normed = ref_norm(stream, gain_ref[...]).astype(jnp.bfloat16)
    n_ref[...] = normed
    queries = dot_last(normed, wq_ref[...]).astype(jnp.bfloat16)
    q_ref[...] = queries
    out = attend_block(
        block, False, False, ql_ref, kl_ref, queries,
        k_ref, vt_ref, kd_ref, s_ref, o_acc, None, lse_ref,
    )
    put_out(out, o_ref, ot_ref)


def ffn_forward_kernel(*refs):
    me_ref, x_ref = refs[:2]
    pieces, weights = refs[2:6], refs[6:10]
    gain_ref, wi_ref, wo_ref, x1_ref, n_ref, hid_ref, act_ref, part_ref = refs[10:18]
    weights_ref, pieces_ref = refs[18:]
    me = me_ref[0]

    @pl.when(pl.program_id(0) == 0)
    def _():
        order_weights(me, weights, weights_ref)

    summed = out_product(me, pieces, slice(None), weights_ref, pieces_ref)
    stream = x_ref[...].astype(jnp.float32) + summed
    x1_ref[...] = stream
    normed = ref_norm(stream, gain_ref[...]).astype(jnp.bfloat16)
    n_ref[...] = normed
    hidden = dot(normed, wi_ref[...])
    hid_ref[...] = hidden
    active = gelu_parts(hidden)[0].astype(jnp.bfloat16)
    act_ref[...] = active
    part_ref[...] = dot(active, wo_ref[...])


def ffn_both_kernel(*refs):
    me_ref, y_ref = refs[:2]
    pieces, weights = refs[2:6], refs[6:10]
    gain_ref, wi_ref, wo_ref, cot_ref = refs[10:14]
    y2_ref, n_ref, act_ref, dhid_ref, part_ref, out_part_ref, weights_ref, pieces_ref = refs[14:]
    me = me_ref[0]

    @pl.when(pl.program_id(0) == 0)
    def _():
        order_weights(me, weights, weights_ref)

    summed = out_product(me, pieces, slice(None), weights_ref, pieces_ref)
    stream = y_ref[...] + summed
    y2_ref[...] = stream
    normed = ref_norm(stream, gain_ref[...]).astype(jnp.bfloat16)
    n_ref[...] = normed
    active, slope = gelu_parts(dot(normed, wi_ref[...]))
    active = active.astype(jnp.bfloat16)
    act_ref[...] = active
    grad = (slope * dot_last(cot_ref[...], wo_ref[...])).astype(jnp.bfloat16)
    dhid_ref[...] = grad
    part_ref[...] = dot_last(grad, wi_ref[...])
    out_part_ref[...] = dot(active, wo_ref[...])


def ffn_backward_kernel(cot_ref, sum_ref, hid_ref, wi_ref, wo_ref, x_ref, g_ref, dhid_ref, part_ref):
    stream = cot_ref[...].astype(jnp.float32) + sum_ref[...]
    x_ref[...] = stream
    branch = stream.astype(jnp.bfloat16)
    g_ref[...] = branch
    slope = gelu_parts(hid_ref[...])[1]
    grad = (slope * dot_last(branch, wo_ref[...])).astype(jnp.bfloat16)
    dhid_ref[...] = grad
    part_ref[...] = dot_last(grad, wi_ref[...])


def half_rows(core, block, mine_ref, sib_ref):
    local = block_rows(lax.rem(block, 2))
    return jnp.where(block // 2 == core, mine_ref[local, :], sib_ref[local, :])


def piece_rows(core, block, refs):
    near, far, near_sib, far_sib = refs
    return half_rows(core, block, near, near_sib) + half_rows(core, block, far, far_sib)


def closing_kernel(x0_ref, eb_ref, egain_ref, z_ref, y0_ref, sb_ref, dgain_ref, s_ref, y2_ref, l_ref,
                   enc_ref, dec_ref, result_ref):
    for start, stream, gain, summed, out in (
        (x0_ref, eb_ref, egain_ref, z_ref, enc_ref), (y0_ref, sb_ref, dgain_ref, s_ref, dec_ref)
    ):
        grad, _ = norm_back(start[...].astype(jnp.float32), gain[...], summed[...])
        out[...] = stream[...] + grad
    result_ref[...] = (y2_ref[...] + l_ref[...]).astype(result_ref.dtype)


def attention_back_kernel(causal, biased, pieces, *refs):
    refs = list(refs)
    take = lambda n: [refs.pop(0) for _ in range(n)]
    core_ref, ql_ref, kl_ref = take(3)
    base_ref, stream_ref = take(2)
    dn_refs = take(pieces)
    gain_ref, wo_ref, q_ref, k_ref, v_ref, o_ref, lse_ref, wq_ref, wk_ref, wv_ref = take(10)
    buckets_ref, table_ref, x0_ref = take(3) if biased else (None, None, None)
    x_ref, g_ref, dq_ref, dk_ref, dv_ref, gain_grad_ref = take(6)
    if biased:
        dtable_ref, own_gain_ref = take(2)
    part_ref = take(1)[0]
    memory_part_ref = None if biased else take(1)[0]
    kt_ref, kd_ref, dq_acc, dk_acc, dv_acc = take(5)
    tiles_ref, grad_ref = take(2) if biased else (None, None)
    block = pl.program_id(0)
    keys, width = k_ref.shape
    heads = width // DK
    core = core_ref[0]
    q_ends = doc_ends(ql_ref)
    scale = jnp.bfloat16(DK ** (-0.5))

    @pl.when(block == 0)
    def _():
        kt_ref[...] = flip(k_ref[...])
        kd_ref[...] = docs_at(
            lax.broadcasted_iota(jnp.int32, (keys, TILE), 0), doc_ends(kl_ref)
        )
        dk_acc[...] = jnp.zeros_like(dk_acc)
        dv_acc[...] = jnp.zeros_like(dv_acc)
        gain_grad_ref[...] = jnp.zeros_like(gain_grad_ref)
        if biased:
            make_tiles(buckets_ref, table_ref, tiles_ref)
            grad_ref[...] = jnp.zeros_like(grad_ref)

    if pieces == 1:
        grad_normed = dn_refs[0][...]
    else:
        grad_normed = piece_rows(core, block, dn_refs)
    grad_in, gain_grad = norm_back(stream_ref[...], gain_ref[...], grad_normed)
    gain_grad_ref[...] += gain_grad
    grad_stream = base_ref[...].astype(jnp.float32) + grad_in
    x_ref[...] = grad_stream
    branch = grad_stream.astype(jnp.bfloat16)
    g_ref[...] = branch
    grads = dot_last(branch, wo_ref[...]).astype(jnp.bfloat16)

    q_docs = docs_at(block * BQ + lax.broadcasted_iota(jnp.int32, (1, BQ), 1), q_ends)
    queries = q_ref[...] * scale
    product = grads.astype(jnp.float32) * o_ref[...].astype(jnp.float32)
    pick = jnp.concatenate(
        [head_mask(h, width).astype(jnp.float32) for h in range(heads)]
        + [jnp.zeros((8 - heads, width), jnp.float32)],
        axis=0,
    )
    inner = lax.dot_general(
        pick,
        product,
        (((1,), (1,)), ((), ())),
        precision=HIGHEST,
        preferred_element_type=jnp.float32,
    )
    q_masked = [queries * head_mask(h, width) for h in range(heads)]
    g_masked = [grads * head_mask(h, width) for h in range(heads)]
    low, high = key_range(ql_ref, q_ends, kl_ref, block, causal)
    dq_acc[...] = jnp.zeros_like(dq_acc)

    @pl.loop(low, high)
    def _(chunk):
        rows = pl.ds(pl.multiple_of(chunk * KC, KC), KC)
        docs = jnp.concatenate([kd_ref[rows, :]] * (BQ // TILE), axis=1)
        allowed = docs == q_docs
        dk = dk_acc[rows, :]
        dv = dv_acc[rows, :]
        for h in range(heads):
            scores = dot_last(k_ref[rows, :], q_masked[h])
            if biased:
                scores = scores + tile_rows(tiles_ref, h, block, chunk, keys)
            scores = jnp.where(allowed, scores, NEG)
            probs = jnp.exp(scores - lse_ref[h : h + 1, :])
            grad_probs = dot_last(v_ref[rows, :], g_masked[h])
            grad_scores = (probs * (grad_probs - inner[h : h + 1, :])).astype(jnp.bfloat16)
            dv = dv + dot(probs.astype(jnp.bfloat16), g_masked[h])
            dk = dk + dot(grad_scores, q_masked[h])
            dq_acc[h * DK : (h + 1) * DK, :] += dot(
                kt_ref[h * DK : (h + 1) * DK, rows], grad_scores
            )
            if biased:
                for t in range(BQ // TILE):
                    start = keys - TILE - TILE * (block * (BQ // TILE) + t) + chunk * KC
                    piece = pl.ds(pl.multiple_of(start, TILE), KC)
                    grad_ref[h, piece, :] += grad_scores[:, t * TILE : (t + 1) * TILE].astype(
                        jnp.float32
                    )
        dk_acc[rows, :] = dk
        dv_acc[rows, :] = dv

    dq = (jnp.transpose(dq_acc[...]) * DK ** (-0.5)).astype(jnp.bfloat16)
    dq_ref[block_rows(block), :] = dq

    @pl.when(block == pl.num_programs(0) - 1)
    def _():
        dk_ref[...] = dk_acc[...].astype(jnp.bfloat16)
        dv_ref[...] = dv_acc[...].astype(jnp.bfloat16)
        own_gain = jnp.zeros(gain_grad_ref.shape, jnp.float32)
        for b in range(keys // ROWS):
            rows = slice(b * ROWS, (b + 1) * ROWS)
            from_q = dot(dq_ref[rows, :], wq_ref[...])
            from_kv = dot(dk_ref[rows, :], wk_ref[...]) + dot(
                dv_ref[rows, :], wv_ref[...]
            )
            if not biased:
                part_ref[rows, :] = from_q
                memory_part_ref[rows, :] = from_kv
                continue
            total = from_q + from_kv
            part_ref[rows, :] = total
            start = x0_ref[rows, :].astype(jnp.float32)
            unit = start * lax.rsqrt(jnp.mean(start * start, axis=-1, keepdims=True) + EPS)
            own_gain = own_gain + jnp.sum(total * unit, axis=0, keepdims=True)
        if biased:
            own_gain_ref[...] = own_gain
            sum_tiles(buckets_ref, grad_ref, dtable_ref)


def whole(shape):
    return pl.BlockSpec(shape, lambda *_: (0,) * len(shape), pipeline_mode=pl.Buffered(1))


def rows_spec(width):
    return pl.BlockSpec((BQ, width), lambda i: (i, 0))


def lanes_spec():
    return pl.BlockSpec((8, BQ), lambda i: (0, i))


SMEM_SPEC = pl.BlockSpec(memory_space=pltpu.SMEM)
BF16, F32 = jnp.bfloat16, jnp.float32


def call(kernel, name, grid, inputs, outputs, scratch, flops, exps=0):
    def size(shape, dtype):
        count = 1
        for dim in shape:
            count *= dim
        return count * jnp.dtype(dtype).itemsize

    moved = sum(size(a.shape, a.dtype) for a, _ in inputs) + sum(size(s, d) for s, d, _ in outputs)
    return pl.pallas_call(
        kernel,
        grid=grid,
        in_specs=[spec for _, spec in inputs],
        out_specs=[spec for _, _, spec in outputs],
        out_shape=[jax.ShapeDtypeStruct(shape, dtype) for shape, dtype, _ in outputs],
        scratch_shapes=scratch,
        compiler_params=pltpu.CompilerParams(
            dimension_semantics=("arbitrary",) * len(grid), vmem_limit_bytes=VMEM_BYTES
        ),
        cost_estimate=pl.CostEstimate(flops=flops // SPEEDUP, bytes_accessed=moved // SPEEDUP, transcendentals=exps // SPEEDUP),
        name=name,
    )(*[a for a, _ in inputs])


def full(array):
    return (array, whole(array.shape))


def attention_scratch(width, keys, biased):
    heads = width // DK
    scratch = [
        pltpu.VMEM((width, keys), BF16),
        pltpu.VMEM((keys, TILE), jnp.int32),
        pltpu.VMEM((heads, keys, BQ), F32),
        pltpu.VMEM((width, BQ), F32),
    ]
    if biased:
        scratch.append(pltpu.VMEM((heads, 2 * keys - TILE, TILE), F32))
    return scratch


def transposed_spec(width):
    return pl.BlockSpec((width, BQ), lambda i: (0, i))


def self_forward(lens, x, gain, wq, wk, wv, bias, causal, name):
    seq, model = x.shape
    width = wq.shape[0]
    inputs = [(lens, SMEM_SPEC)]
    inputs += [full(a) for a in (x, gain, wq, wk, wv, bias[0], bias[1])]
    outputs = [((seq, model), BF16, whole((seq, model)))]
    outputs += [((seq, width), BF16, whole((seq, width)))] * 3
    outputs += [((seq, width), BF16, rows_spec(width)), ((8, seq), F32, lanes_spec())]
    outputs.append(((width, seq), F32, transposed_spec(width)))
    result = call(
        functools.partial(self_forward_kernel, causal), name, (seq // BQ,), inputs, outputs,
        attention_scratch(width, seq, True), 6 * seq * model * width + 2 * seq * seq * width,
        seq * seq,
    )
    return result[:6], result[6]


def order_scratch(width, model, rows):
    return [pltpu.VMEM((4, width, model), BF16), pltpu.VMEM((4, width, rows), F32)]


def piece_inputs(pieces, weights, model, half):
    width = pieces[0].shape[0]
    spec = pl.BlockSpec((width, model), lambda *_: (0, half), pipeline_mode=pl.Buffered(1))
    return [(a, transposed_spec(width)) for a in pieces] + [(a, spec) for a in weights]


def cross_forward(me, ql, kl, y0, pieces, weights, x1, enc_sum, gain, wq, wk, wv):
    seq, model = y0.shape
    width = wq.shape[0]
    inputs = [(me, SMEM_SPEC), (ql, SMEM_SPEC), (kl, SMEM_SPEC), (y0, rows_spec(model))]
    inputs += piece_inputs(pieces, weights, model, 0)
    inputs += [full(a) for a in (x1, enc_sum, gain, wq, wk, wv)]
    outputs = [
        ((seq, model), F32, rows_spec(model)),
        ((seq, model), BF16, rows_spec(model)),
        ((seq, model), BF16, whole((seq, model))),
        ((seq, width), BF16, rows_spec(width)),
        ((seq, width), BF16, whole((seq, width))),
        ((seq, width), BF16, whole((seq, width))),
        ((seq, width), BF16, rows_spec(width)),
        ((8, seq), F32, lanes_spec()),
        ((width, seq), F32, transposed_spec(width)),
    ]
    scratch = attention_scratch(width, seq, False) + order_scratch(width, model, ROWS)
    result = call(
        cross_forward_kernel, "cross_forward", (seq // BQ,), inputs, outputs, scratch,
        14 * seq * model * width + 2 * seq * seq * width, seq * seq,
    )
    return result[:8], result[8]


def row_outputs(seq, *kinds):
    return [((seq, width), dtype, rows_spec(width)) for width, dtype in kinds]


def ffn_forward(me, x, pieces, weights, gain, wi, wo):
    seq, model = x.shape
    units = wi.shape[1]
    inputs = [(me, SMEM_SPEC), (x, rows_spec(model))] + piece_inputs(pieces, weights, model, 0)
    inputs += [full(a) for a in (gain, wi, wo)]
    outputs = row_outputs(seq, (model, F32), (model, BF16), (units, F32), (units, BF16), (model, F32))
    return call(
        ffn_forward_kernel, "ffn_forward", (seq // ROWS,), inputs, outputs,
        order_scratch(weights[0].shape[0], model, ROWS), 6 * seq * model * units, seq * units,
    )


def ffn_both(me, y, pieces, weights, gain, wi, wo, cot):
    seq, model = y.shape
    units = wi.shape[1]
    inputs = [(me, SMEM_SPEC), (y, rows_spec(model))] + piece_inputs(pieces, weights, model, 1)
    inputs += [full(a) for a in (gain, wi, wo)] + [(cot, rows_spec(model))]
    outputs = row_outputs(
        seq, (model, F32), (model, BF16), (units, BF16), (units, BF16), (model, F32), (model, F32)
    )
    return call(
        ffn_both_kernel, "ffn_both", (seq // ROWS,), inputs, outputs,
        order_scratch(weights[0].shape[0], model, ROWS), 10 * seq * model * units, seq * units,
    )


def ffn_backward(cot, summed, hid, wi, wo):
    seq, units = hid.shape
    model = wi.shape[0]
    inputs = [(cot, rows_spec(model)), (summed, rows_spec(model)), (hid, rows_spec(units))]
    inputs += [full(wi), full(wo)]
    outputs = row_outputs(seq, (model, F32), (model, BF16), (units, BF16), (model, F32))
    return call(
        ffn_backward_kernel, "ffn_backward", (seq // ROWS,), inputs, outputs, [],
        4 * seq * model * units, seq * units,
    )


def closing(x0, eb, enc_gain, enc_sum, y0, sb, dec_gain, dec_sum, y2, last):
    seq, model = x0.shape
    inputs = [
        full(a) if a.shape[0] == 1 else (a, rows_spec(model))
        for a in (x0, eb, enc_gain, enc_sum, y0, sb, dec_gain, dec_sum, y2, last)
    ]
    return call(
        closing_kernel, "closing", (seq // ROWS,), inputs,
        row_outputs(seq, (model, F32), (model, F32), (model, BF16)), [], 20 * seq * model,
    )


def dot_rows(left, right):
    return lax.dot_general(
        left, right, (((0,), (0,)), ((), ())), preferred_element_type=jnp.float32
    )


def attention_weights_kernel(dq_ref, dk_ref, dv_ref, o_ref, n_ref, m_ref, g_ref, out_ref):
    count = dq_ref.shape[1]
    pairs = ((dq_ref, n_ref), (dk_ref, m_ref), (dv_ref, m_ref), (o_ref, g_ref))
    for i, (left, right) in enumerate(pairs):
        out_ref[i * count : (i + 1) * count, :] = dot_rows(left[...], right[...])


def attention_weights(grads, attended, normed, memory):
    seq, model = normed.shape
    width = attended.shape[1]
    inputs = [full(a) for a in (*grads[2:5], attended, normed, memory, grads[1])]
    outputs = [((4 * width, model), F32, whole((4 * width, model)))]
    return call(
        attention_weights_kernel, "attention_weights", (1,), inputs, outputs, [],
        8 * seq * model * width,
    )[0]


def attention_back(
    core, ql, kl, base, stream, dn, gain, wo, kept, wq, wk, wv, bias, x0, causal, name
):
    q, k, v, o, lse = kept
    seq, width = q.shape
    model = wo.shape[1]
    heads = width // DK
    biased = bias is not None
    inputs = [(core, SMEM_SPEC), (ql, SMEM_SPEC), (kl, SMEM_SPEC)]
    inputs += [(base, rows_spec(model)), (stream, rows_spec(model))]
    inputs += [(dn[0], rows_spec(model))] if len(dn) == 1 else [full(a) for a in dn]
    inputs += [full(gain), full(wo)]
    inputs += [(q, rows_spec(width)), full(k), full(v), (o, rows_spec(width)), (lse, lanes_spec())]
    inputs += [full(wq), full(wk), full(wv)]
    if biased:
        inputs += [full(bias[0]), full(bias[1]), full(x0)]
    outputs = [((seq, model), F32, rows_spec(model)), ((seq, model), BF16, rows_spec(model))]
    outputs += [((seq, width), BF16, whole((seq, width)))] * 3
    outputs.append(((1, model), F32, whole((1, model))))
    if biased:
        outputs.append((bias[1].shape, F32, whole(bias[1].shape)))
        outputs.append(((1, model), F32, whole((1, model))))
    outputs.append(((seq, model), F32, whole((seq, model))))
    if not biased:
        outputs.append(((seq, model), F32, whole((seq, model))))
    scratch = [
        pltpu.VMEM((width, seq), BF16),
        pltpu.VMEM((seq, TILE), jnp.int32),
        pltpu.VMEM((width, BQ), F32),
        pltpu.VMEM((seq, width), F32),
        pltpu.VMEM((seq, width), F32),
    ]
    if biased:
        scratch += [pltpu.VMEM((heads, 2 * seq - TILE, TILE), F32)] * 2
    result = call(
        functools.partial(attention_back_kernel, causal, biased, len(dn)),
        name, (seq // BQ,), inputs,
        outputs, scratch, 8 * seq * model * width + 5 * seq * seq * width, seq * seq,
    )
    return result[:6], result[6:]


MESH_ID = pl.DeviceIdType.MESH
MB_PER_ROW = 0.768 * 4 / 1000
RATES = (2.0, 21.0, 21.3, 21.5, 44.0)
DEPTH = 2


class Copies:
    def __init__(self, send_sem, recv_sem):
        self.send_sem, self.recv_sem = send_sem, recv_sem
        self.all, self.steps, self.first = [], [], []

    def copy(self, source, target, axis, index, link, rows, stage=0):
        i = len(self.all)

        def make():
            return pltpu.make_async_remote_copy(
                src_ref=source,
                dst_ref=target,
                send_sem=self.send_sem.at[i],
                recv_sem=self.recv_sem.at[i],
                device_id={axis: index},
                device_id_type=MESH_ID,
            )

        self.all.append((make, link, rows, stage))
        return i

    def step(self, waits, work, starts):
        self.steps.append((waits, work, starts))

    def start(self, i):
        make, link, rows, _ = self.all[i]
        self.made[i] = make()
        self.made[i].start()
        begin = max(self.now, self.free.get(link, 0.0))
        if link == 4:
            half = 22.0 * rows * MB_PER_ROW
            begin = max(begin, self.free.get(3, 0.0) - half)
            self.free[3] = max(self.free.get(3, 0.0), begin) + half
        self.free[link] = begin + RATES[link] * rows * MB_PER_ROW
        self.arrive[i] = self.free[link] + 1.0

    def fill(self):
        for i in sorted(self.pending, key=lambda i: (-self.all[i][3], i)):
            link = self.all[i][1]
            busy = sum(self.all[j][1] == link and self.arrive[j] > self.now for j in self.made)
            if busy < DEPTH or link < 2:
                self.pending.remove(i)
                self.start(i)

    def run(self):
        self.now, self.free, self.arrive, self.made = 0.0, {}, {}, {}
        self.pending = list(self.first)
        left = list(self.steps)
        self.fill()
        while left:
            ready = [s for s in left if all(i in self.made for i in s[0])]
            step = min(ready, key=lambda s: max([self.arrive[i] for i in s[0]], default=0.0))
            left.remove(step)
            for i in step[0]:
                self.made[i].wait_recv()
                self.now = max(self.now, self.arrive[i])
            if step[1] is not None:
                step[1]()
            self.pending += step[2]
            self.fill()
        for made in self.made.values():
            made.wait_send()


def mp_partners():
    me = lax.axis_index("mp")
    core = lax.rem(me, 2)
    return core, me + 1 - 2 * core, lax.rem(me + 2, 4)


def dp_side(bit):
    return lax.rem(lax.axis_index("dp") // (1 << bit), 2)


def dp_partner(bit):
    return lax.axis_index("dp") + (1 << bit) * (1 - 2 * dp_side(bit))


def greet(bits):
    barrier = pltpu.get_barrier_semaphore()
    _, beside, across = mp_partners()
    ids = [{"mp": beside}, {"mp": across}] + [{"dp": dp_partner(bit)} for bit in bits]
    for device_id in ids:
        pl.semaphore_signal(barrier, inc=1, device_id=device_id, device_id_type=MESH_ID)
    pl.semaphore_wait(barrier, len(ids))


def rows_at(start, count):
    return pl.ds(pl.multiple_of(start, 8), count)


def mp_job(copies, part_ref, near_ref, far_ref, out_ref, chunks, finish=None, far=True):
    core, beside, across = mp_partners()
    count = part_ref.shape[0] // (2 * chunks)

    def one(k):
        mine = rows_at((2 * k + core) * count, count)
        other = rows_at((2 * k + 1 - core) * count, count)
        first = copies.copy(part_ref.at[other, :], near_ref.at[k], "mp", beside, 0, count)
        copies.first.append(first)

        def add_near():
            near_ref[k] = part_ref[mine, :] + near_ref[k]

        second = copies.copy(near_ref.at[k], far_ref.at[k], "mp", across, 1, count)
        copies.step([first], add_near, [second])

        def add_far():
            out_ref[mine, :] = near_ref[k] + far_ref[k]
            if finish is not None:
                finish(mine)

        third = copies.copy(out_ref.at[mine, :], out_ref.at[mine, :], "mp", beside, 0, count)
        copies.step([second], add_far, [third])
        copies.step([third], None if finish is None else lambda: finish(other), [])

    for k in range(chunks):
        one(k)


def near_job(copies, part_ref, land_ref, out_ref):
    core, beside, _ = mp_partners()
    count = part_ref.shape[0] // 2
    mine = rows_at(core * count, count)
    other = rows_at((1 - core) * count, count)
    first = copies.copy(part_ref.at[other, :], land_ref, "mp", beside, 0, count)
    copies.first.append(first)

    def add():
        out_ref[...] = part_ref[mine, :] + land_ref[...]

    copies.step([first], add, [])


LINKS = (2, 3, 4)


def scatter_job(copies, part_ref, land_refs, bits, base, rows, store, got_ref=None):
    start, count, waits, work = base, rows, None, None
    source, origin = part_ref, 0
    for level, bit in enumerate(bits):
        count = count // 2
        side = dp_side(bit)
        keep = start + side * count
        give = start + (1 - side) * count
        land = land_refs[level]
        place = base // rows * count
        landing = slice(place, place + count)
        got = land
        if level == 0 and got_ref is not None:
            made, got = None, got_ref
        else:
            made = copies.copy(
                source.at[rows_at(give - origin, count), :], land.at[landing, :], "dp",
                dp_partner(bit), LINKS[min(bit, 2)], count, level,
            )
            if level == 0:
                copies.first.append(made)
            else:
                copies.step(waits, work, [made])

        def work(
            source=source, origin=origin, keep=keep, land=land, got=got, landing=landing, count=count
        ):
            land[landing, :] = source[rows_at(keep - origin, count), :] + got[landing, :]

        waits = [] if made is None else [made]
        source, origin, start = land, keep - place, keep

    def last(add=work, land=land, landing=landing, start=start, count=count):
        add()
        store(start, count, land[landing, :])

    return waits, last


def gather_job(copies, out_ref, bits, base, rows, waits, work):
    count = rows >> len(bits)
    start, size = base, rows
    for bit in bits:
        size = size // 2
        start = start + dp_side(bit) * size
    for level, bit in enumerate(reversed(bits)):
        held = rows_at(start, count)
        made = copies.copy(
            out_ref.at[held, :], out_ref.at[held, :], "dp", dp_partner(bit),
            LINKS[min(bit, 2)], count, len(bits) + level,
        )
        if waits is None:
            work()
            copies.first.append(made)
        else:
            copies.step(waits, work, [made])
        waits, work = [made], None
        start = start - dp_side(bit) * count
        count = count * 2
    copies.step(waits, None, [])


def small_job(copies, small_ref, land_ref, held_ref, out_ref, bits, shared):
    core, beside, across = mp_partners()
    hops = [("mp", beside, 0), ("mp", across, 1)]
    hops += [("dp", dp_partner(bit), LINKS[min(bit, 2)]) for bit in bits]
    count = small_ref.shape[0]
    first_rows = lax.broadcasted_iota(jnp.int32, small_ref.shape, 0) < shared
    source, waits, work = small_ref, None, None
    for i, (axis, index, link) in enumerate(hops):
        made = copies.copy(source, land_ref.at[i], axis, index, link, count)
        if i == 0:
            copies.first.append(made)
        else:
            copies.step(waits, work, [made])

        def work(i=i, source=source, last=i == len(hops) - 1):
            got = land_ref[i]
            if i < 2:
                got = jnp.where(first_rows, got, 0.0)
            target = out_ref if last else held_ref.at[i]
            target[...] = source[...] + got

        waits, source = [made], held_ref.at[i]
    copies.step(waits, work, [])


CHUNKS = 4
PIECES = 4


def sums(number, parts=(), near=(), scatter=(), gather=(), units=(), turns=(), halves=(), small=None, shared=0):
    bits = list(range((lax.axis_size("dp") - 1).bit_length()))
    turned = bits[1:] + bits[:1]
    dp = bool(scatter or gather or units or small is not None)
    smalls = [] if small is None else [small]
    inputs = [*parts, *near, *scatter, *gather, *units, *smalls, *halves]
    model = inputs[0].shape[1]
    shares = lax.axis_size("dp")
    outputs = [(a.shape, F32) for a in parts]
    outputs += [((a.shape[0] // 2, model), F32) for a in near]
    outputs += [((a.shape[0] // shares, model), F32) for a in scatter]
    outputs += [((a.shape[0] * shares, model), F32) for a in gather]
    outputs += [(a.shape, F32) for a in (*units, *smalls)]
    lands = []
    chunks = 2 * CHUNKS if len(parts) == 1 else CHUNKS
    for a in parts:
        lands += [pltpu.VMEM((chunks, a.shape[0] // (2 * chunks), model), F32)] * 2
    for a in near:
        lands.append(pltpu.VMEM((a.shape[0] // 2, model), F32))
    for a in (*scatter, *units):
        lands += [pltpu.VMEM((a.shape[0] >> (i + 1), model), F32) for i in range(len(bits))]
    for a in smalls:
        lands += [pltpu.VMEM((2 + len(bits), *a.shape), F32)] * 2
    count, ends = len(inputs), len(inputs) + len(outputs)
    total = 3 * chunks * len(parts) + len(near) + len(smalls) * (2 + len(bits))
    total += len(bits) * PIECES * (len(scatter) + len(gather) + 2 * len(units))

    def kernel(*refs):
        ins, outs = list(refs[:count]), list(refs[count:ends])
        scratch = list(refs[ends:-2])
        half_refs = [None] * (len(units) - len(halves)) + ins[count - len(halves) :]
        greet(bits if dp else [])
        copies = Copies(refs[-2], refs[-1])
        for _ in parts:
            mp_job(copies, ins.pop(0), scratch.pop(0), scratch.pop(0), outs.pop(0), chunks)
        for _ in near:
            near_job(copies, ins.pop(0), scratch.pop(0), outs.pop(0))
        for a in scatter:
            part_ref, out_ref = ins.pop(0), outs.pop(0)
            land_refs = [scratch.pop(0) for _ in bits]
            rows = a.shape[0] // PIECES
            for piece in range(PIECES):

                def keep(start, count, value, piece=piece, out_ref=out_ref):
                    out_ref[piece * count : (piece + 1) * count, :] = value

                waits, work = scatter_job(
                    copies, part_ref, land_refs, bits, piece * rows, rows, keep
                )
                copies.step(waits, work, [])
        for a in gather:
            part_ref, out_ref = ins.pop(0), outs.pop(0)
            rows = a.shape[0] * shares // PIECES
            for piece in range(PIECES):
                start, size = piece * rows, rows
                for bit in bits:
                    size = size // 2
                    start = start + dp_side(bit) * size

                def put(start=start, size=size, piece=piece, part_ref=part_ref, out_ref=out_ref):
                    out_ref[rows_at(start, size), :] = part_ref[
                        piece * size : (piece + 1) * size, :
                    ]

                gather_job(copies, out_ref, bits, piece * rows, rows, None, put)
        for a, half_ref in zip(units, half_refs):
            part_ref, out_ref = ins.pop(0), outs.pop(0)
            land_refs = [scratch.pop(0) for _ in bits]
            rows = a.shape[0] // PIECES
            for piece in range(PIECES):

                def keep(start, count, value, out_ref=out_ref):
                    out_ref[rows_at(start, count), :] = value

                order = turned if piece in turns else bits
                waits, work = scatter_job(
                    copies, part_ref, land_refs, order, piece * rows, rows, keep, half_ref
                )
                gather_job(copies, out_ref, order, piece * rows, rows, waits, work)
        if small is not None:
            small_job(copies, ins[0], scratch[0], scratch[1], outs[0], bits, shared)
        copies.run()

    result = pl.pallas_call(
        kernel,
        in_specs=[whole(a.shape) for a in inputs],
        out_specs=[whole(shape) for shape, _ in outputs],
        out_shape=[jax.ShapeDtypeStruct(shape, dtype) for shape, dtype in outputs],
        grid=(1,),
        scratch_shapes=lands
        + [pltpu.SemaphoreType.DMA((total,)), pltpu.SemaphoreType.DMA((total,))],
        compiler_params=pltpu.CompilerParams(
            collective_id=number, has_side_effects=True, vmem_limit_bytes=VMEM_BYTES
        ),
        cost_estimate=pl.CostEstimate(flops=1, bytes_accessed=1, transcendentals=0),
        name="sums",
    )(*inputs)
    groups = []
    for group in (parts, near, scatter, gather, units, smalls):
        groups.append(list(result[: len(group)]))
        result = result[len(group) :]
    return groups


def first_half(unit):
    rows = unit.shape[0] // (2 * PIECES)
    pieces = unit.reshape(PIECES, 2, rows, unit.shape[1])
    other = 1 - lax.rem(lax.axis_index("dp"), 2)
    return lax.dynamic_index_in_dim(pieces, other, 1, False).reshape(PIECES * rows, -1)


def first_swap(value):
    pairs = [(i, i ^ 1) for i in range(lax.axis_size("dp"))]
    return lax.ppermute(value, "dp", pairs)


def shares_fit(rows):
    return rows % (8 * PIECES * lax.axis_size("dp")) == 0


CORE_SWAP = [(0, 1), (1, 0), (2, 3), (3, 2)]
CHIP_SWAP = [(0, 2), (2, 0), (1, 3), (3, 1)]


def core_swap(value):
    return lax.ppermute(value, "mp", CORE_SWAP)


def chip_swap(value):
    return lax.ppermute(value, "mp", CHIP_SWAP)


def part(value, start, rows):
    return lax.dynamic_slice_in_dim(value, start, rows, axis=0)


class Chain:
    def __init__(self):
        self.token = None

    def tie(self, value):
        if self.token is None:
            return value
        value, _ = lax.optimization_barrier((value, self.token))
        return value

    def mark(self, value):
        self.token = value


class Wire:
    def __init__(self, chain, swap):
        self.chain, self.swap = chain, swap

    def send(self, value):
        self.value = self.swap(self.chain.tie(value))

    def wait(self):
        self.value = self.chain.tie(self.value)
        self.chain.mark(self.value)
        return self.value


class Gather:
    def __init__(self, chain):
        self.chain = chain
        self.y, self.s, self.r = [Wire(chain, swap) for swap in (chip_swap, core_swap, core_swap)]

    def put(self, own):
        self.own = own

    def sy(self):
        self.y.send(self.own)

    def wy(self):
        self.y.wait()

    def ss(self):
        self.s.send(self.own)

    def ws(self):
        self.s.wait()

    def sr(self):
        self.r.send(self.y.value)

    def wr(self):
        self.r.wait()

    def pieces(self):
        return (self.own, self.y.value, self.s.value, self.r.value)


def project_weight(left, right):
    return lax.dot_general(
        left, right, (((0,), (0,)), ((), ())), preferred_element_type=jnp.float32
    )


def signed_buckets(buckets, seq):
    fill = jnp.full((2 * seq - buckets.shape[0],), -1, jnp.int32)
    return jnp.concatenate([fill, buckets])[None, :]


def body(
    encoder_input,
    decoder_input,
    encoder_lengths,
    decoder_lengths,
    encoder_buckets,
    decoder_buckets,
    encoder_attn_gain,
    encoder_query,
    encoder_key,
    encoder_value,
    encoder_output,
    encoder_bias,
    encoder_ffn_gain,
    encoder_ffn_in,
    encoder_ffn_out,
    decoder_attn_gain,
    decoder_query,
    decoder_key,
    decoder_value,
    decoder_output,
    decoder_bias,
    cross_gain,
    cross_query,
    cross_key,
    cross_value,
    cross_output,
    decoder_ffn_gain,
    decoder_ffn_in,
    decoder_ffn_out,
    encoder_cotangent,
    decoder_cotangent,
):
    _, seq, width = encoder_input.shape
    enc_lens, dec_lens = encoder_lengths, decoder_lengths
    enc_bias = (signed_buckets(encoder_buckets, seq), encoder_bias)
    dec_bias = (signed_buckets(decoder_buckets, seq), decoder_bias)
    me = lax.axis_index("mp").astype(jnp.int32).reshape(1)
    core = lax.rem(me, 2)
    x0, y0 = encoder_input[0], decoder_input[0]
    enc_cot, dec_cot = encoder_cotangent[0], decoder_cotangent[0]
    row = lambda gain: gain[None, :]
    encoder_query, encoder_key, encoder_value = encoder_query.T, encoder_key.T, encoder_value.T
    decoder_query, decoder_key, decoder_value = decoder_query.T, decoder_key.T, decoder_value.T
    cross_query, cross_key, cross_value = cross_query.T, cross_key.T, cross_value.T
    chain = Chain()
    tie, mark = chain.tie, chain.mark

    wide_e, wide, e, d, x = [Gather(chain) for _ in range(5)]
    wide_e.put(encoder_output.astype(F32))
    mark(wide_e.own)
    wide_e.sy()
    count = encoder_output.shape[0] // lax.axis_size("dp")
    place = lax.axis_index("dp") * count
    slices = Wire(chain, chip_swap)
    slices.send(
        jnp.concatenate(
            [part(decoder_output, place, count), part(cross_output, place, count)], axis=1
        ).astype(F32)
    )
    enc, out = self_forward(
        enc_lens, tie(x0), row(encoder_attn_gain), encoder_query, encoder_key, encoder_value,
        enc_bias, False, "encoder_attention",
    )
    mark(out)
    e.put(out)
    wide_e.wy()
    slices.wait()
    e.sy()
    e.ss()
    wide.y.value = lax.all_gather(tie(slices.value), "dp", axis=0, tiled=True)
    wide_e.sr()
    wide_e.ss()

    dec, out = self_forward(
        dec_lens, tie(y0), row(decoder_attn_gain), decoder_query, decoder_key, decoder_value,
        dec_bias, True, "decoder_attention",
    )
    mark(out)
    d.put(out)
    e.wy()
    e.sr()
    d.sy()
    e.ws()
    wide_e.ws()
    wide_e.wr()
    e.wr()
    own = jnp.concatenate([decoder_output, cross_output], axis=1).astype(F32)
    wide.put(own)

    ffn = ffn_forward(
        me, tie(x0), e.pieces(), wide_e.pieces(), row(encoder_ffn_gain), encoder_ffn_in,
        encoder_ffn_out,
    )
    mark(ffn[4])
    d.wy()
    d.ss()
    d.sr()
    wide.ss()
    enc_sum = sums(1, parts=[tie(ffn[4])])[0][0]
    mark(enc_sum)
    wide.sr()
    d.ws()
    d.wr()
    wide.ws()
    wide.wr()

    cross, out = cross_forward(
        me, dec_lens, enc_lens, tie(y0), d.pieces(), wide.pieces(), ffn[0], enc_sum, row(cross_gain),
        cross_query, cross_key, cross_value,
    )
    mark(out)
    x.put(out)
    x.sy()
    x.ss()
    x.wy()
    x.sr()
    x.ws()
    x.wr()

    both = ffn_both(
        me, tie(cross[0]), x.pieces(), wide.pieces(), row(decoder_ffn_gain), decoder_ffn_in,
        decoder_ffn_out, dec_cot,
    )
    mark(both[4])
    dn = sums(2, parts=[tie(both[4])])[0][0]
    mark(dn)

    cb, (own_part, memory_part) = attention_back(
        core, dec_lens, enc_lens, dec_cot, both[0], (tie(dn),), row(decoder_ffn_gain),
        cross_output, cross[3:8], cross_query, cross_key, cross_value, None, None, False,
        "cross_back",
    )
    mark(own_part)
    unit_1a = project_weight(tie(both[1]), both[3])
    unit_1b = project_weight(both[2], dec_cot)
    unit_2 = attention_weights((*cb[:2], tie(cb[2]), *cb[3:]), cross[6], cross[1], cross[2])
    mark(unit_2)
    unit_1a = tie(unit_1a)
    mark(unit_1a)
    unit_1a, unit_1b, unit_2 = lax.psum((unit_1a, unit_1b, unit_2), "dp")
    split_units = shares_fit(width)
    totals, nears, _, _, _, _ = sums(3, parts=[tie(memory_part)], near=[own_part])
    grad_memory, own_near = totals[0], nears[0]
    mark(grad_memory)

    back = ffn_backward(enc_cot, tie(grad_memory), ffn[2], encoder_ffn_in, encoder_ffn_out)
    mark(back[3])
    unit_4a = project_weight(tie(ffn[1]), back[2])
    mark(unit_4a)
    unit_4b = project_weight(tie(ffn[3]), back[1])
    mark(unit_4b)
    dn = sums(4, parts=[tie(back[3])])[0][0]
    mark(dn)
    half_4b, half_5 = [Wire(chain, first_swap) for _ in range(2)]
    half_4b.send(first_half(unit_4b))
    own_far, own_beside, own_relay = [
        Wire(chain, swap) for swap in (chip_swap, core_swap, core_swap)
    ]
    own_far.send(own_near)
    own_beside.send(own_near)

    eb, (enc_table, enc_gain, enc_part) = attention_back(
        core, enc_lens, enc_lens, back[0], ffn[0], (tie(dn),), row(encoder_ffn_gain),
        encoder_output, enc[1:6], encoder_query, encoder_key, encoder_value, enc_bias, x0, False,
        "encoder_back",
    )
    mark(enc_part)
    own_beside.wait()
    unit_5 = attention_weights((*eb[:2], tie(eb[2]), *eb[3:]), enc[4], enc[0], enc[0])
    mark(unit_5)
    own_far.wait()
    own_relay.send(own_far.value)
    half_4b.wait()
    half_5.send(first_half(unit_5))
    own_relay.wait()

    own_pieces = (own_near, own_far.value, own_beside.value, own_relay.value)
    sb, (dec_table, dec_gain, dec_part) = attention_back(
        core, dec_lens, dec_lens, tie(cb[0]), cross[0], own_pieces, row(cross_gain),
        decoder_output, dec[1:6], decoder_query, decoder_key, decoder_value, dec_bias, y0, True,
        "decoder_back",
    )
    mark(dec_part)
    unit_3 = attention_weights((*sb[:2], tie(sb[2]), *sb[3:]), dec[4], dec[0], dec[0])
    mark(unit_3)
    half_5.wait()
    tables = []
    for table in (enc_table, dec_table):
        flat = table.reshape(1, -1)
        tables.append(jnp.pad(flat, ((0, 0), (0, width - flat.shape[1]))))
    blank = jnp.zeros((1, width), F32)
    small = jnp.concatenate([enc_gain, dec_gain, eb[5], sb[5], cb[5], *tables, blank], axis=0)
    units = [unit_3, unit_4a, unit_4b, unit_5] if split_units else []
    halves = [half_4b.value, half_5.value] if split_units else []
    totals, _, _, _, units, smalls = sums(
        5, parts=[enc_part, dec_part, both[5]], units=units, halves=halves,
        small=small, shared=2
    )
    small = smalls[0]
    if split_units:
        unit_3, unit_4a, unit_4b, unit_5 = units
    else:
        unit_4a, unit_3, unit_4b, unit_5 = lax.psum((unit_4a, unit_3, unit_4b, unit_5), "dp")
    enc_grad, dec_grad, result = closing(
        x0, eb[0], row(encoder_attn_gain), totals[0], y0, sb[0], row(decoder_attn_gain), totals[1],
        both[0], totals[2],
    )

    def matrices(stack):
        count = stack.shape[0] // 4
        pieces = [stack[i * count : (i + 1) * count] for i in range(4)]
        return [jnp.transpose(piece) for piece in pieces[:3]] + pieces[3:]

    shape = encoder_bias.shape
    count = shape[0] * shape[1]
    return (
        cross[2][None],
        result[None],
        enc_grad[None],
        dec_grad[None],
        small[0],
        *matrices(unit_5),
        small[5, :count].reshape(shape),
        small[2],
        unit_4a,
        unit_4b,
        small[1],
        *matrices(unit_3),
        small[6, :count].reshape(shape),
        small[3],
        *matrices(unit_2),
        small[4],
        unit_1a,
        unit_1b,
    )


def solution(mesh):
    return jax.shard_map(
        body,
        mesh=mesh,
        in_specs=(
            P("dp", None, None),
            P("dp", None, None),
            P("dp", None),
            P("dp", None),
            P(),
            P(),
            P(),
            P(None, "mp"),
            P(None, "mp"),
            P(None, "mp"),
            P("mp", None),
            P(None, "mp"),
            P(),
            P(None, "mp"),
            P("mp", None),
            P(),
            P(None, "mp"),
            P(None, "mp"),
            P(None, "mp"),
            P("mp", None),
            P(None, "mp"),
            P(),
            P(None, "mp"),
            P(None, "mp"),
            P(None, "mp"),
            P("mp", None),
            P(),
            P(None, "mp"),
            P("mp", None),
            P("dp", None, None),
            P("dp", None, None),
        ),
        out_specs=(
            P("dp", None, None),
            P("dp", None, None),
            P("dp", None, None),
            P("dp", None, None),
            P(),
            P(None, "mp"),
            P(None, "mp"),
            P(None, "mp"),
            P("mp", None),
            P(None, "mp"),
            P(),
            P(None, "mp"),
            P("mp", None),
            P(),
            P(None, "mp"),
            P(None, "mp"),
            P(None, "mp"),
            P("mp", None),
            P(None, "mp"),
            P(),
            P(None, "mp"),
            P(None, "mp"),
            P(None, "mp"),
            P("mp", None),
            P(),
            P(None, "mp"),
            P("mp", None),
        ),
        check_vma=False,
    )
```
